256 devices in a mesh: grp: 16 (over y, x_hi, core), dom: 16 (over z, x_lo).
Axes of the slice: x: 4 (x_hi: 2, x_lo: 2; x = x_hi * 2 + x_lo), y: 4, z: 8, core: 2. Of those that a mesh axis runs over, the one named last changes fastest.
Arguments:
- queries: bfloat16 [65536, 256], P(('grp', 'dom')), may hold values from -6 to 6
- key_rows: bfloat16 [65536, 256], P(('grp', 'dom')), may hold values from -6 to 6
- value_rows: bfloat16 [65536, 256], P(('grp', 'dom')), may hold values from -6 to 6
- saved_output: bfloat16 [65536, 256], P(('grp', 'dom')), may hold values from -6 to 6
- output_grad: bfloat16 [65536, 256], P(('grp', 'dom')), may hold values from -24 to 24
- log_norm: float32 [8, 65536], P(None, ('grp', 'dom')), may hold values from 5 to 8
- local_lists: int32 [512, 32], P(('grp', 'dom')), may hold values from 0 to 31, as said below
- expander_lists: int32 [512, 16], P(('grp', 'dom')), may hold values from 0 to 31, as said below
- local_counts: int32 [512], P(('grp', 'dom')), may hold values from 1 to 32, as said below
- expander_counts: int32 [512], P(('grp', 'dom')), may hold values from 1 to 16, as said below
Outputs:
- query_grad: bfloat16 [65536, 256], P(('grp', 'dom'))
- key_grad: bfloat16 [65536, 256], P(('grp', 'dom'))
- value_grad: bfloat16 [65536, 256], P(('grp', 'dom'))
The draws below stay inside these ranges and needn't reach their ends.
Inputs may be any that keep to these rules, and one draw needn't show every extreme that they name: `local_lists`: each row is an ordering of all 32 blocks of the partition. `expander_lists`: entries of a row are distinct and never name the block's own partition. `local_counts`: some block uses its whole list. `expander_counts`: some block uses its whole list.
All inputs are finite; a program needn't handle non-finite values.
Results may differ from the reference program's by a relative error of at most 0.0054.
Values may be sent and summed in bfloat16 or wider, within the bound.
A program may use at most 128 MiB of HBM per device.

```python
import math
import jax
import jax.numpy as jnp
from jax import lax

HEADS = 8
HEAD_DIM = 32
D = 256
BLOCK = 128
BLOCKS_DEV = 2
NUM_BLOCKS = 512
NODES = 65536
LOCAL_SLOTS = 32
FAR_SLOTS = 16
N_GRP = 16
N_DOM = 16


def skewed_counts(key, most):
    first, second, third = jax.random.split(key, 3)
    lower = jax.random.randint(first, (NUM_BLOCKS,), 1, most + 1)
    upper = jax.random.randint(second, (NUM_BLOCKS,), 1, most + 1)
    counts = (lower * upper + most - 1) // most
    chosen = jax.random.randint(third, (), 0, NUM_BLOCKS)
    return counts.at[chosen].set(most).astype(jnp.int32)


def draw_local_lists(key, part):
    key = jax.random.fold_in(key, 11)
    streams = jax.random.split(key, NUM_BLOCKS)
    return jax.vmap(lambda single: jax.random.permutation(single, LOCAL_SLOTS))(streams).astype(jnp.int32)


def draw_expander_lists(key, part):
    key = jax.random.fold_in(key, 12)
    streams = jax.random.split(key, NUM_BLOCKS)
    picked = jax.vmap(lambda single: jax.random.permutation(single, (N_DOM - 1) * BLOCKS_DEV)[:FAR_SLOTS])(streams)
    blocks = jnp.arange(NUM_BLOCKS, dtype=jnp.int32)
    home = blocks // BLOCKS_DEV % N_DOM
    other = picked // BLOCKS_DEV
    other = other + (other >= home[:, None]).astype(jnp.int32)
    return (other * BLOCKS_DEV + picked % BLOCKS_DEV).astype(jnp.int32)


def draw_local_counts(key, part):
    key = jax.random.fold_in(key, 13)
    return skewed_counts(key, LOCAL_SLOTS)


def draw_expander_counts(key, part):
    key = jax.random.fold_in(key, 14)
    return skewed_counts(key, FAR_SLOTS)


def levels(key, extent, cuts, smallest, largest):
    loudness, own = 1.0, jax.random.fold_in(key, 6)
    for dim, shards_of in cuts:
        heights = jnp.exp(jax.random.uniform(jax.random.fold_in(own, dim), (shards_of,), jnp.float32, smallest / len(cuts), largest / len(cuts)))
        loudness = loudness * jnp.repeat(heights, extent[dim] // shards_of).reshape([-1 if axis == dim else 1 for axis in range(len(extent))])
    return loudness


def normal_values(key, shape, deviation, limit, cuts=(), kind=jnp.bfloat16):
    drawn = jax.random.normal(key, shape, jnp.float32) * deviation
    if len(cuts) > 0:
        drawn = levels(key, shape, cuts, -0.22, 0.18) * drawn
    return jnp.clip(drawn, min=-limit, max=limit).astype(kind)


def setup_inputs(seed: int = 0) -> dict:
    splits = jax.random.split(jax.random.key(seed), 11)
    return {
        "queries": normal_values(splits[0], (NODES, D), 1.0, 6.0, ((0, 256),)),
        "key_rows": normal_values(splits[1], (NODES, D), 1.0, 6.0, ((0, 256),)),
        "value_rows": normal_values(splits[2], (NODES, D), 1.0, 6.0, ((0, 256),)),
        "saved_output": normal_values(splits[3], (NODES, D), 1.0, 6.0, ((0, 256),)),
        "output_grad": normal_values(splits[4], (NODES, D), 4.0, 24.0, ((0, 256),)),
        "log_norm": jnp.clip(5.0 + 3.0 * jax.random.uniform(splits[5], (HEADS, NODES), jnp.float32) ** levels(splits[5], (HEADS, NODES), ((1, 256),), -0.2, 0.2), 5.0, 8.0),
        "local_lists": draw_local_lists(jax.random.fold_in(splits[10], 71), 0),
        "expander_lists": draw_expander_lists(jax.random.fold_in(splits[10], 71), 0),
        "local_counts": draw_local_counts(jax.random.fold_in(splits[10], 71), 0),
        "expander_counts": draw_expander_counts(jax.random.fold_in(splits[10], 71), 0),
    }


def reference(queries, key_rows, value_rows, saved_output, output_grad, log_norm, local_lists, expander_lists, local_counts, expander_counts):
    total_blocks = BLOCKS_DEV * N_GRP * N_DOM
    blocks = jnp.arange(total_blocks, dtype=jnp.int32)
    device = blocks // BLOCKS_DEV
    rank = device // N_DOM
    domain = device % N_DOM
    local_ids = (local_lists // BLOCKS_DEV * N_DOM + domain[:, None]) * BLOCKS_DEV + local_lists % BLOCKS_DEV
    far_ids = (rank[:, None] * N_DOM + expander_lists // BLOCKS_DEV) * BLOCKS_DEV + expander_lists % BLOCKS_DEV
    neighbours = jnp.concatenate([local_ids, far_ids], axis=1).astype(jnp.int32)
    local_live = jnp.arange(LOCAL_SLOTS, dtype=jnp.int32)[None, :] < local_counts[:, None]
    far_live = jnp.arange(FAR_SLOTS, dtype=jnp.int32)[None, :] < expander_counts[:, None]
    visible = jnp.concatenate([local_live, far_live], axis=1).astype(jnp.float32)
    shape4 = (total_blocks, BLOCK, HEADS, HEAD_DIM)
    query4 = queries.astype(jnp.float32).reshape(shape4)
    key4 = key_rows.astype(jnp.float32).reshape(shape4)
    value4 = value_rows.astype(jnp.float32).reshape(shape4)
    grad4 = output_grad.astype(jnp.float32).reshape(shape4)
    delta3 = lax.optimization_barrier(jnp.sum(grad4 * saved_output.astype(jnp.float32).reshape(shape4), axis=3)).transpose(0, 2, 1)
    lse3 = log_norm.astype(jnp.float32).reshape(HEADS, total_blocks, BLOCK).transpose(1, 0, 2)
    scaling = 1.0 / math.sqrt(HEAD_DIM)

    def advance(carry, slot):
        grad_q, grad_k, grad_v = carry
        ids, shown = slot
        near_keys = key4[ids]
        near_values = value4[ids]
        scores = jnp.einsum('bqhd,bkhd->bhqk', query4, near_keys)
        attention = jnp.exp(scaling * scores - lse3[:, :, :, None]) * shown[:, None, None, None]
        attention_low = lax.optimization_barrier(attention.astype(jnp.bfloat16)).astype(jnp.float32)
        grad_v = grad_v.at[ids].add(jnp.einsum('bhqk,bqhd->bkhd', attention_low, grad4))
        grad_p = jnp.einsum('bqhd,bkhd->bhqk', grad4, near_values)
        score_grad = (attention * (grad_p - delta3[:, :, :, None])).astype(jnp.bfloat16)
        score_grad = lax.optimization_barrier(score_grad).astype(jnp.float32)
        grad_q = grad_q + scaling * jnp.einsum('bhqk,bkhd->bqhd', score_grad, near_keys)
        grad_k = grad_k.at[ids].add(scaling * jnp.einsum('bhqk,bqhd->bkhd', score_grad, query4))
        return ((grad_q, grad_k, grad_v), None)
    start = (jnp.zeros(shape4, jnp.float32), jnp.zeros(shape4, jnp.float32), jnp.zeros(shape4, jnp.float32))
    (grad_q, grad_k, grad_v), _ = lax.scan(advance, start, (neighbours.T, visible.T))
    flat = (total_blocks * BLOCK, HEADS * HEAD_DIM)
    return (grad_q.reshape(flat).astype(jnp.bfloat16), grad_k.reshape(flat).astype(jnp.bfloat16), grad_v.reshape(flat).astype(jnp.bfloat16))
```

```python
import functools
import math

import jax
import jax.numpy as jnp
from jax import lax
from jax.experimental import pallas as pl
from jax.experimental.pallas import tpu as pltpu
from jax.sharding import PartitionSpec as P

HEADS = 8
HEAD_DIM = 32
BLOCK = 128
ROWS = 256
D = 256
N_Z, N_Y = 8, 4
Q_DEVS = N_Z + N_Y
K_DEVS = 6
SCALING = 1.0 / math.sqrt(HEAD_DIM)
LOG2E = math.log2(math.e)
MESH = pl.DeviceIdType.MESH
ANY = pl.BlockSpec(memory_space=pl.ANY)
VMEM = pl.BlockSpec(memory_space=pltpu.VMEM)
SMEM = pl.BlockSpec(memory_space=pltpu.SMEM)
VMEM_LIMIT = 56 * 1024 * 1024


def places():
    g, m = lax.axis_index("grp"), lax.axis_index("dom")
    return g // 4, g // 2 % 2, g % 2, m // 2, m % 2


def partners(y, xh, c, z, xl):
    def at(y=y, xh=xh, c=c, z=z, xl=xl):
        return ((y * 2 + xh) * 2 + c, z * 2 + xl)

    return {
        "right": at(z=(z + 1) % N_Z),
        "left": at(z=(z + N_Z - 1) % N_Z),
        "y1": at(y=(y + 1) % N_Y),
        "y2": at(y=(y + 2) % N_Y),
        "y3": at(y=(y + 3) % N_Y),
        "far_x": at(xh=1 - xh),
        "near_x": at(xl=1 - xl),
        "sibling": at(c=1 - c),
    }


def meet(others):
    barrier = pltpu.get_barrier_semaphore()
    for device in others.values():
        pl.semaphore_signal(barrier, inc=1, device_id=device, device_id_type=MESH)
    pl.semaphore_wait(barrier, len(others))


def gather_kernel(
    q_ref, g_ref, o_ref, k_ref, v_ref, lse_ref, ll_ref, el_ref, lc_ref, ec_ref,
    allq, allg, meta, vis, allk, allv,
    gbuf, obuf, mbuf, vbuf, in_sem, own_sem,
    right_send, right_recv, left_send, left_recv, y_send, y_recv, x_send, x_recv,
):
    y, xh, c, z, xl = places()
    others = partners(y, xh, c, z, xl)
    loads = [
        pltpu.make_async_copy(g_ref, gbuf, in_sem.at[0]),
        pltpu.make_async_copy(o_ref, obuf, in_sem.at[1]),
    ]
    for load in loads:
        load.start()
    own_pairs = [
        (q_ref, allq.at[z]), (q_ref, allq.at[N_Z + y]),
        (g_ref, allg.at[z]), (g_ref, allg.at[N_Z + y]),
        (k_ref, allk.at[xl]), (k_ref, allk.at[2 + xh * 2 + c]),
        (v_ref, allv.at[xl]), (v_ref, allv.at[2 + xh * 2 + c]),
        (mbuf, meta.at[z]), (mbuf, meta.at[N_Z + y]),
        (vbuf, vis.at[z]), (vbuf, vis.at[N_Z + y]),
    ]
    own = [pltpu.make_async_copy(a, b, own_sem.at[i]) for i, (a, b) in enumerate(own_pairs)]

    def remote(src, dst, send, recv, who):
        return pltpu.make_async_remote_copy(
            src_ref=src, dst_ref=dst, send_sem=send, recv_sem=recv,
            device_id=others[who], device_id_type=MESH,
        )

    mine = [q_ref, g_ref, mbuf, vbuf]
    whole = [allq, allg, meta, vis]
    halves = [BLOCK, BLOCK, HEADS, None]

    def ring(hop, kind, way):
        origin = (z + N_Z - hop) % N_Z if way == "right" else (z + hop) % N_Z
        src = mine[kind] if hop == 0 else whole[kind].at[origin]
        dst = whole[kind].at[origin]
        if hop == 3:
            half = halves[kind]
            if half is None:
                if way == "left":
                    return None
            else:
                rows = pl.ds(0 if way == "right" else half, half)
                src, dst = src.at[rows], dst.at[rows]
        send, recv = (right_send, right_recv) if way == "right" else (left_send, left_recv)
        return remote(src, dst, send.at[hop, kind], recv.at[hop, kind], way)

    rings = {(h, k, w): ring(h, k, w) for h in range(4) for k in range(4) for w in ("right", "left")}
    ys = {
        (k, step): remote(
            mine[k], whole[k].at[N_Z + y], y_send.at[step - 1, k], y_recv.at[step - 1, k], f"y{step}"
        )
        for k in range(4) for step in (1, 2, 3)
    }
    place = 2 + xh * 2 + c
    other_place = 2 + (1 - xh) * 2 + c
    xs = {}
    for i, (src, dst) in enumerate(((k_ref, allk), (v_ref, allv))):
        xs["far_x", i] = remote(src, dst.at[place], x_send.at[0, i], x_recv.at[0, i], "far_x")
        xs["near_x", i] = remote(src, dst.at[xl], x_send.at[1, i], x_recv.at[1, i], "near_x")
        xs["sibling", i] = remote(src, dst.at[place], x_send.at[2, i], x_recv.at[2, i], "sibling")
        xs["onward", i] = remote(
            dst.at[other_place], dst.at[other_place], x_send.at[3, i], x_recv.at[3, i], "sibling"
        )

    def begin(kind):
        for way in ("right", "left"):
            rings[0, kind, way].start()

    def begin_y(kind):
        for step in (1, 3, 2):
            ys[kind, step].start()

    meet(others)
    begin(0)
    begin(1)
    for i in range(2):
        xs["far_x", i].start()
        begin_y(i)
        xs["near_x", i].start()
        xs["sibling", i].start()
    for i in range(8):
        own[i].start()

    lane = lax.broadcasted_iota(jnp.int32, (8, 128), 1)

    def mark(lists, counts, e, base):
        def one(s, seen):
            hit = (lane == base + lists[e, s]) & (s < counts[e])
            return jnp.where(hit, 1, seen)
        return one

    seen = jnp.zeros((8, 128), jnp.int32)
    for e in range(2):
        seen = lax.fori_loop(0, ll_ref.shape[1], mark(ll_ref, lc_ref, e, e * 64), seen)
        seen = lax.fori_loop(0, el_ref.shape[1], mark(el_ref, ec_ref, e, e * 64 + 32), seen)
    vbuf[...] = seen
    begin(3)
    begin_y(3)
    for load in loads:
        load.wait()
    product = gbuf[...].astype(jnp.float32) * obuf[...].astype(jnp.float32)
    high = product.astype(jnp.bfloat16)
    low = (product - high.astype(jnp.float32)).astype(jnp.bfloat16)
    rows_of = lax.broadcasted_iota(jnp.int32, (HEADS, D), 0)
    cols_of = lax.broadcasted_iota(jnp.int32, (HEADS, D), 1)
    pick = jnp.where(cols_of // HEAD_DIM == rows_of, 1.0, 0.0).astype(jnp.bfloat16)
    dims = (((1,), (1,)), ((), ()))
    delta = lax.dot_general(pick, high, dims, preferred_element_type=jnp.float32)
    delta = delta + lax.dot_general(pick, low, dims, preferred_element_type=jnp.float32)
    mbuf[0:HEADS, :] = lse_ref[...] * LOG2E
    mbuf[HEADS:, :] = delta
    begin(2)
    begin_y(2)
    for i in range(8, 12):
        own[i].start()

    for hop in range(1, 4):
        for kind in (0, 1, 3, 2):
            for way in ("right", "left"):
                rings[hop - 1, kind, way].wait_recv()
                if rings[hop, kind, way] is not None:
                    rings[hop, kind, way].start()
        if hop == 2:
            for i in range(2):
                xs["far_x", i].wait_recv()
                xs["onward", i].start()
    for kind in range(4):
        for way in ("right", "left"):
            if rings[3, kind, way] is not None:
                rings[3, kind, way].wait_recv()
    for copy in ys.values():
        copy.wait()
    for (who, i), copy in xs.items():
        if who == "far_x":
            copy.wait_send()
        else:
            copy.wait()
    for copy in rings.values():
        if copy is not None:
            copy.wait_send()
    for copy in own:
        copy.wait()


def gather(q, g, o, k, v, lse, ll, el, lc, ec):
    bf16 = jnp.bfloat16
    dma = pltpu.SemaphoreType.DMA
    return pl.pallas_call(
        gather_kernel,
        name="gather",
        out_shape=(
            jax.ShapeDtypeStruct((Q_DEVS, ROWS, D), bf16),
            jax.ShapeDtypeStruct((Q_DEVS, ROWS, D), bf16),
            jax.ShapeDtypeStruct((Q_DEVS, 2 * HEADS, ROWS), jnp.float32),
            jax.ShapeDtypeStruct((Q_DEVS, 8, 128), jnp.int32),
            jax.ShapeDtypeStruct((K_DEVS, ROWS, D), bf16),
            jax.ShapeDtypeStruct((K_DEVS, ROWS, D), bf16),
        ),
        in_specs=[ANY] * 5 + [VMEM] + [SMEM] * 4,
        out_specs=[ANY] * 6,
        scratch_shapes=[
            pltpu.VMEM((ROWS, D), bf16),
            pltpu.VMEM((ROWS, D), bf16),
            pltpu.VMEM((2 * HEADS, ROWS), jnp.float32),
            pltpu.VMEM((8, 128), jnp.int32),
            dma((2,)), dma((12,)),
            dma((4, 4)), dma((4, 4)), dma((4, 4)), dma((4, 4)),
            dma((3, 4)), dma((3, 4)), dma((4, 2)), dma((4, 2)),
        ],
        compiler_params=pltpu.CompilerParams(
            collective_id=0, has_side_effects=True, vmem_limit_bytes=VMEM_LIMIT
        ),
    )(q, g, o, k, v, lse, ll, el, lc, ec)


def pairs_kernel(
    vis, allq, allg, meta, allk, allv, dq_ref, dk_ref, dv_ref, qbd, gbd, kt, dqa, dka, dva
):
    y, _, _, z, _ = places()
    f32, bf16 = jnp.float32, jnp.bfloat16
    dqa[...] = jnp.zeros_like(dqa)
    dka[...] = jnp.zeros_like(dka)
    dva[...] = jnp.zeros_like(dva)
    head_of = lax.broadcasted_iota(jnp.int32, (1, 128), 1) // HEAD_DIM
    masks = [jnp.where(head_of == h, 1.0, 0.0).astype(bf16) for h in range(4)]
    across = (((1,), (1,)), ((), ()))
    along = (((1,), (0,)), ((), ()))

    def turn(d, carry):
        kt[d] = allk[d].astype(f32).T.astype(bf16)
        return carry

    lax.fori_loop(0, K_DEVS, turn, 0)

    def dot(a, b, dims):
        return lax.dot_general(a, b, dims, preferred_element_type=f32)

    def query_block(n, carry):
        qd, e = n // 2, n % 2
        far = qd < N_Z
        base = e * 64 + jnp.where(far, 32 + z * 4, y * 8)
        number = jnp.where(far, 4, 8)
        first = jnp.where(far, 0, 4)
        live = lax.fori_loop(0, number, lambda j, t: t + vis[qd, 0, base + j], 0)
        rows = pl.ds(pl.multiple_of(e * BLOCK, BLOCK), BLOCK)

        @pl.when(live > 0)
        def _():
            for u in range(2):
                qh = allq[qd, rows, u * 128:(u + 1) * 128]
                gh = allg[qd, rows, u * 128:(u + 1) * 128]
                for h in range(4):
                    at = (u * 4 + h) * BLOCK
                    qbd[at:at + BLOCK, :] = qh * masks[h]
                    gbd[at:at + BLOCK, :] = gh * masks[h]

            def key_block(j, carry):
                @pl.when(vis[qd, 0, base + j] > 0)
                def _():
                    kd, ke = (first + j) // 2, (first + j) % 2
                    krows = pl.ds(pl.multiple_of(ke * BLOCK, BLOCK), BLOCK)
                    for p in range(4):
                        cols = slice(p // 2 * 128, p // 2 * 128 + 128)
                        qt = qbd[p * 256:(p + 1) * 256, :]
                        gt = gbd[p * 256:(p + 1) * 256, :]
                        lse = jnp.concatenate(
                            [meta[qd, 2 * p:2 * p + 1, rows], meta[qd, 2 * p + 1:2 * p + 2, rows]], axis=1
                        )
                        delta = jnp.concatenate(
                            [
                                meta[qd, HEADS + 2 * p:HEADS + 2 * p + 1, rows],
                                meta[qd, HEADS + 2 * p + 1:HEADS + 2 * p + 2, rows],
                            ],
                            axis=1,
                        )
                        scores = dot(allk[kd, krows, cols], qt, across)
                        attention = jnp.exp2(scores * (SCALING * LOG2E) - lse)
                        grad_p = dot(allv[kd, krows, cols], gt, across)
                        score_grad = (attention * (grad_p - delta)).astype(bf16)
                        dva[kd, krows, cols] += dot(attention.astype(bf16), gt, along)
                        dka[kd, krows, cols] += dot(score_grad, qt, along)
                        turned = dot(kt[kd, p * 64:(p + 1) * 64, krows], score_grad, along)
                        dqa[qd, p * 64:p * 64 + 32, rows] += turned[0:32, 0:128]
                        dqa[qd, p * 64 + 32:p * 64 + 64, rows] += turned[32:64, 128:256]

                return carry

            lax.fori_loop(0, number, key_block, 0)

        return carry

    lax.fori_loop(0, 2 * Q_DEVS, query_block, 0)
    for d in range(Q_DEVS):
        dq_ref[d] = (dqa[d] * SCALING).astype(bf16)
    for d in range(K_DEVS):
        dk_ref[d] = (dka[d] * SCALING).astype(bf16)
        dv_ref[d] = dva[d].astype(bf16)


def pairs(vis, allq, allg, meta, allk, allv):
    bf16, f32 = jnp.bfloat16, jnp.float32
    return pl.pallas_call(
        pairs_kernel,
        name="pairs",
        out_shape=(
            jax.ShapeDtypeStruct((Q_DEVS, D, ROWS), bf16),
            jax.ShapeDtypeStruct((K_DEVS, ROWS, D), bf16),
            jax.ShapeDtypeStruct((K_DEVS, ROWS, D), bf16),
        ),
        in_specs=[SMEM] + [VMEM] * 5,
        out_specs=[VMEM] * 3,
        scratch_shapes=[
            pltpu.VMEM((HEADS * BLOCK, 128), bf16),
            pltpu.VMEM((HEADS * BLOCK, 128), bf16),
            pltpu.VMEM((K_DEVS, D, ROWS), bf16),
            pltpu.VMEM((Q_DEVS, D, ROWS), f32),
            pltpu.VMEM((K_DEVS, ROWS, D), f32),
            pltpu.VMEM((K_DEVS, ROWS, D), f32),
        ],
        compiler_params=pltpu.CompilerParams(vmem_limit_bytes=VMEM_LIMIT),
    )(vis, allq, allg, meta, allk, allv)


def scatter_kernel(
    dq, dk, dv, qg_ref, kg_ref, vg_ref,
    right_out, left_out, right_in, left_in, y_in, near_in, sib_in, pass_in, far_out, far_in,
    right_send, right_recv, left_send, left_recv, y_send, y_recv, x_send, x_recv,
):
    y, xh, c, z, xl = places()
    others = partners(y, xh, c, z, xl)
    f32, bf16 = jnp.float32, jnp.bfloat16

    def remote(src, dst, send, recv, who):
        copy = pltpu.make_async_remote_copy(
            src_ref=src, dst_ref=dst, send_sem=send, recv_sem=recv,
            device_id=others[who], device_id_type=MESH,
        )
        copy.start()
        return copy

    meet(others)
    top, bottom = slice(0, BLOCK), slice(BLOCK, 2 * BLOCK)
    rights, lefts = [], []
    rights.append(remote(
        dq.at[(z + 4) % N_Z, pl.ds(0, BLOCK)], right_in.at[0, pl.ds(0, BLOCK)],
        right_send.at[0], right_recv.at[0], "right"))
    lefts.append(remote(
        dq.at[(z + 4) % N_Z, pl.ds(BLOCK, BLOCK)], left_in.at[0, pl.ds(BLOCK, BLOCK)],
        left_send.at[0], left_recv.at[0], "left"))
    place = 2 + xh * 2 + c
    sib_place = 2 + xh * 2 + (1 - c)
    pass_place = 2 + (1 - xh) * 2 + (1 - c)
    far_place = 2 + (1 - xh) * 2 + c
    xs = {}
    for i, part in enumerate((dk, dv)):
        xs["pass", i] = remote(part.at[pass_place], pass_in.at[i], x_send.at[0, i], x_recv.at[0, i], "sibling")
    for i, part in enumerate((dk, dv)):
        xs["sib", i] = remote(part.at[sib_place], sib_in.at[i], x_send.at[1, i], x_recv.at[1, i], "sibling")
        xs["near", i] = remote(part.at[1 - xl], near_in.at[i], x_send.at[2, i], x_recv.at[2, i], "near_x")
    ys = [
        remote(dq.at[N_Z + (y + step) % N_Y], y_in.at[step - 1], y_send.at[step - 1], y_recv.at[step - 1], f"y{step}")
        for step in (1, 2, 3)
    ]
    for i, part in enumerate((dk, dv)):
        xs["pass", i].wait_recv()
        far_out[i] = (part[far_place].astype(f32) + pass_in[i].astype(f32)).astype(bf16)
        xs["far", i] = remote(far_out.at[i], far_in.at[i], x_send.at[3, i], x_recv.at[3, i], "far_x")
    for step in (1, 2, 3):
        to_right, to_left = (z + 4 - step) % N_Z, (z + 4 + step) % N_Z
        rights[step - 1].wait_recv()
        if step == 1:
            right_out[0, top] = (dq[to_right, top].astype(f32) + right_in[0, top].astype(f32)).astype(bf16)
            right_out[0, bottom] = dq[to_right, bottom]
        else:
            right_out[step - 1] = (dq[to_right].astype(f32) + right_in[step - 1].astype(f32)).astype(bf16)
        rights.append(remote(
            right_out.at[step - 1], right_in.at[step], right_send.at[step], right_recv.at[step], "right"))
        lefts[step - 1].wait_recv()
        if step == 1:
            left_out[0, bottom] = (dq[to_left, bottom].astype(f32) + left_in[0, bottom].astype(f32)).astype(bf16)
            left_out[0, top] = dq[to_left, top]
        else:
            left_out[step - 1] = (dq[to_left].astype(f32) + left_in[step - 1].astype(f32)).astype(bf16)
        lefts.append(remote(
            left_out.at[step - 1], left_in.at[step], left_send.at[step], left_recv.at[step], "left"))
    for i, (part, out) in enumerate(((dk, kg_ref), (dv, vg_ref))):
        total = part[xl].astype(f32) + part[place].astype(f32)
        for who, held in (("near", near_in), ("sib", sib_in), ("far", far_in)):
            xs[who, i].wait_recv()
            total = total + held[i].astype(f32)
        out[...] = total.astype(bf16)
    total = dq[z].astype(f32) + dq[N_Z + y].astype(f32)
    for i in range(3):
        ys[i].wait_recv()
        total = total + y_in[i].astype(f32)
    rights[3].wait_recv()
    lefts[3].wait_recv()
    total = total + right_in[3].astype(f32) + left_in[3].astype(f32)
    qg_ref[...] = total.T.astype(bf16)
    for copy in rights + lefts + ys + list(xs.values()):
        copy.wait_send()


def scatter(dq, dk, dv):
    bf16 = jnp.bfloat16
    dma = pltpu.SemaphoreType.DMA
    tile = (ROWS, D)
    return pl.pallas_call(
        scatter_kernel,
        name="scatter",
        out_shape=[jax.ShapeDtypeStruct(tile, bf16)] * 3,
        in_specs=[VMEM] * 3,
        out_specs=[VMEM] * 3,
        scratch_shapes=[
            pltpu.VMEM((3, *tile), bf16), pltpu.VMEM((3, *tile), bf16),
            pltpu.VMEM((4, *tile), bf16), pltpu.VMEM((4, *tile), bf16),
            pltpu.VMEM((3, *tile), bf16), pltpu.VMEM((2, *tile), bf16),
            pltpu.VMEM((2, *tile), bf16), pltpu.VMEM((2, *tile), bf16),
            pltpu.VMEM((2, *tile), bf16), pltpu.VMEM((2, *tile), bf16),
            dma((4,)), dma((4,)), dma((4,)), dma((4,)),
            dma((3,)), dma((3,)), dma((4, 2)), dma((4, 2)),
        ],
        compiler_params=pltpu.CompilerParams(
            collective_id=1, has_side_effects=True, vmem_limit_bytes=VMEM_LIMIT
        ),
    )(dq, dk, dv)


def body(
    queries, key_rows, value_rows, saved_output, output_grad, log_norm,
    local_lists, expander_lists, local_counts, expander_counts,
):
    allq, allg, meta, vis, allk, allv = gather(
        queries, output_grad, saved_output, key_rows, value_rows, log_norm,
        local_lists, expander_lists, local_counts, expander_counts,
    )
    dq, dk, dv = pairs(vis, allq, allg, meta, allk, allv)
    return tuple(scatter(dq, dk, dv))


def solution(mesh):
    rows = P(("grp", "dom"), None)
    flat = P(("grp", "dom"))
    return jax.shard_map(
        body,
        mesh=mesh,
        in_specs=(rows, rows, rows, rows, rows, P(None, ("grp", "dom")), rows, rows, flat, flat),
        out_specs=(rows, rows, rows),
        check_vma=False,
    )
```

```python
import math

import jax
import jax.numpy as jnp
from jax import lax
from jax.experimental import pallas as pl
from jax.experimental.pallas import tpu as pltpu
from jax.sharding import PartitionSpec as P

HEADS = 8
HEAD_DIM = 32
BLOCK = 128
ROWS = 256
D = 256
N_Z, N_Y = 8, 4
Q_SLOTS = 11
K_SLOTS = 5
META = 24
HIDE = 1e30
SCALING = 1.0 / math.sqrt(HEAD_DIM)
LOG2E = math.log2(math.e)
MESH = pl.DeviceIdType.MESH
ANY = pl.BlockSpec(memory_space=pl.ANY)
VMEM = pl.BlockSpec(memory_space=pltpu.VMEM)
SMEM = pl.BlockSpec(memory_space=pltpu.SMEM)
VMEM_LIMIT = 56 * 1024 * 1024
FAR, NEAR, ACROSS = 0, 1, 2
STEPS = (
    (0, NEAR), (0, FAR), (1, FAR), (7, FAR), (8, NEAR), (0, ACROSS), (8, ACROSS), (2, FAR),
    (6, FAR), (4, FAR), (3, FAR), (5, FAR), (10, ACROSS), (9, ACROSS), (10, NEAR), (9, NEAR),
)
KEY_SLOTS = {FAR: (0, 1), NEAR: (0, 2), ACROSS: (3, 4)}
NT = (((1,), (1,)), ((), ()))
NN = (((1,), (0,)), ((), ()))


def dot(a, b, dims):
    return lax.dot_general(a, b, dims, preferred_element_type=jnp.float32)


def places():
    g, m = lax.axis_index("grp"), lax.axis_index("dom")
    return g // 4, g // 2 % 2, g % 2, m // 2, m % 2


def partners(y, xh, c, z, xl):
    def at(y=y, xh=xh, c=c, z=z, xl=xl):
        return ((y * 2 + xh) * 2 + c, z * 2 + xl)

    return {
        "right": at(z=(z + 1) % N_Z),
        "left": at(z=(z + N_Z - 1) % N_Z),
        "y1": at(y=(y + 1) % N_Y),
        "y2": at(y=(y + 2) % N_Y),
        "y3": at(y=(y + 3) % N_Y),
        "far_x": at(xh=1 - xh),
        "near_x": at(xl=1 - xl),
        "sibling": at(c=1 - c),
    }


def meet(others):
    barrier = pltpu.get_barrier_semaphore()
    for device in others.values():
        pl.semaphore_signal(barrier, inc=1, device_id=device, device_id_type=MESH)
    pl.semaphore_wait(barrier, len(others))


def kernel(
    q_ref, g_ref, o_ref, k_ref, v_ref, lse_ref, ll_ref, el_ref, lc_ref, ec_ref,
    qg_ref, kg_ref, vg_ref,
    qb, gb, ob, qt, gt, meta, kk, vv, km, vm, kt, dqa, dka, dva,
    ring_out, ring_in, y_out, y_in, x_out, x_in,
    in_sem, ring_send, ring_recv, y_send, y_recv, x_send, x_recv,
    rr_send, rr_recv, ry_send, ry_recv, rx_send, rx_recv,
):
    y, xh, c, z, xl = places()
    others = partners(y, xh, c, z, xl)
    f32, bf16 = jnp.float32, jnp.bfloat16

    def remote(src, dst, send, recv, who):
        return pltpu.make_async_remote_copy(
            src_ref=src, dst_ref=dst, send_sem=send, recv_sem=recv,
            device_id=others[who], device_id_type=MESH,
        )

    held = (qt, gt, meta)
    halves = ((0, BLOCK), (0, BLOCK), (0, 16))
    sizes = ((BLOCK, BLOCK), (BLOCK, BLOCK), (16, 8))

    def ring(hop, kind, way):
        whole = held[kind]
        src, dst = ((N_Z - hop) % N_Z, N_Z - 1 - hop) if way == 0 else (hop, hop + 1)
        src, dst = whole.at[src], whole.at[dst]
        if hop == 3:
            start = 0 if way == 0 else sizes[kind][0]
            rows = pl.ds(start, sizes[kind][way])
            src, dst = src.at[rows], dst.at[rows]
        return remote(
            src, dst, ring_send.at[hop, kind, way], ring_recv.at[hop, kind, way],
            "right" if way == 0 else "left",
        )

    def ycopy(step, kind):
        whole = held[kind]
        return remote(
            whole.at[0], whole.at[N_Z - 1 + N_Y - step], y_send.at[step - 1, kind],
            y_recv.at[step - 1, kind], f"y{step}",
        )

    def xcopy(what, i):
        whole, own = (kk, k_ref) if i == 0 else (vv, v_ref)
        number, who = {"near": (0, "near_x"), "sib": (1, "sibling"), "far": (2, "far_x"), "on": (3, "sibling")}[what]
        src = whole.at[3] if what == "on" else own
        return remote(src, whole.at[number + 1], x_send.at[number, i], x_recv.at[number, i], who)

    def ring_back(hop, way):
        buf, into = ring_out.at[hop, way], ring_in.at[hop, way]
        if hop == 0:
            rows = pl.ds(0 if way == 0 else BLOCK, BLOCK)
            buf, into = buf.at[rows], into.at[rows]
        return remote(buf, into, rr_send.at[hop, way], rr_recv.at[hop, way], "right" if way == 0 else "left")

    def y_back(step):
        return remote(y_out.at[step - 1], y_in.at[step - 1], ry_send.at[step - 1], ry_recv.at[step - 1], f"y{step}")

    def x_back(what, i):
        number, who = {"near": (0, "near_x"), "sib": (1, "sibling"), "pass": (2, "sibling"), "far": (3, "far_x")}[what]
        return remote(x_out.at[number, i], x_in.at[number, i], rx_send.at[number, i], rx_recv.at[number, i], who)

    loads = [
        pltpu.make_async_copy(src, dst, in_sem.at[i])
        for i, (src, dst) in enumerate(
            ((q_ref, qb), (g_ref, gb), (o_ref, ob), (k_ref, kk.at[0]), (v_ref, vv.at[0]))
        )
    ]
    for load in loads:
        load.start()

    lane = lax.broadcasted_iota(jnp.int32, (8, 128), 1)

    def mark(lists, counts, e, base):
        def one(s, hidden):
            hit = (lane == base + lists[e, s]) & (s < counts[e])
            return jnp.where(hit, 0.0, hidden)
        return one

    hidden = jnp.full((8, 128), HIDE, f32)
    for e in range(2):
        hidden = lax.fori_loop(0, ll_ref.shape[1], mark(ll_ref, lc_ref, e, e * 64), hidden)
        hidden = lax.fori_loop(0, el_ref.shape[1], mark(el_ref, ec_ref, e, e * 64 + 32), hidden)
    meta[0, 16:24, 0:128] = hidden
    meta[0, 16:24, 128:256] = hidden
    meta[0, 0:HEADS, :] = lse_ref[...] * LOG2E

    meet(others)
    for i in range(2):
        for what in ("near", "sib", "far"):
            xcopy(what, i).start()
    loads[0].wait()
    qt[0] = qb[...].astype(f32).T.astype(bf16)
    for way in range(2):
        ring(0, 0, way).start()
    for step in (1, 3):
        ycopy(step, 0).start()
    loads[1].wait()
    gt[0] = gb[...].astype(f32).T.astype(bf16)
    for way in range(2):
        ring(0, 1, way).start()
    for step in (1, 3):
        ycopy(step, 1).start()
    loads[2].wait()
    product = gb[...].astype(f32) * ob[...].astype(f32)
    high = product.astype(bf16)
    low = (product - high.astype(f32)).astype(bf16)
    rows_of = lax.broadcasted_iota(jnp.int32, (HEADS, D), 0)
    cols_of = lax.broadcasted_iota(jnp.int32, (HEADS, D), 1)
    pick = jnp.where(cols_of // HEAD_DIM == rows_of, 1.0, 0.0).astype(bf16)
    meta[0, HEADS:2 * HEADS, :] = dot(pick, high, NT) + dot(pick, low, NT)
    for way in range(2):
        ring(0, 2, way).start()
    for step in (1, 3):
        ycopy(step, 2).start()
    for kind in range(3):
        ycopy(2, kind).start()

    dqa[...] = jnp.zeros_like(dqa)
    dka[...] = jnp.zeros_like(dka)
    dva[...] = jnp.zeros_like(dva)
    head_of = lax.broadcasted_iota(jnp.int32, (1, 128), 1) // HEAD_DIM
    masks = [jnp.where(head_of == h, 1.0, 0.0).astype(bf16) for h in range(4)]

    def spread(slot):
        kt[slot] = kk[slot].astype(f32).T.astype(bf16)
        for h in range(HEADS):
            cols = slice(h // 4 * 128, h // 4 * 128 + 128)
            km[slot, h] = kk[slot, :, cols] * masks[h % 4]
            vm[slot, h] = vv[slot, :, cols] * masks[h % 4]

    def arrive(what):
        for i in range(2):
            xcopy(what, i).wait_recv()

    def pass_on(hop):
        for kind in range(3):
            for way in range(2):
                ring(hop - 1, kind, way).wait_recv()
                ring(hop, kind, way).start()

    def y_arrive(step):
        for kind in range(3):
            ycopy(step, kind).wait_recv()

    def send_back(hop):
        for way in range(2):
            slot = 4 - hop if way == 0 else 4 + hop
            if hop == 0:
                rows = slice(0, BLOCK) if way == 0 else slice(BLOCK, ROWS)
                ring_out[0, way, rows] = (dqa[slot, rows] * SCALING).astype(bf16)
            else:
                ring_back(hop - 1, way).wait_recv()
                if hop == 1:
                    rows, rest = slice(0, BLOCK), slice(BLOCK, ROWS)
                    if way == 1:
                        rows, rest = rest, rows
                    ring_out[1, way, rows] = (
                        dqa[slot, rows] * SCALING + ring_in[0, way, rows].astype(f32)
                    ).astype(bf16)
                    ring_out[1, way, rest] = (dqa[slot, rest] * SCALING).astype(bf16)
                else:
                    ring_out[hop, way] = (
                        dqa[slot] * SCALING + ring_in[hop - 1, way].astype(f32)
                    ).astype(bf16)
            ring_back(hop, way).start()

    def y_send_back(step):
        y_out[step - 1] = (dqa[N_Z - 1 + step] * SCALING).astype(bf16)
        y_back(step).start()

    def x_send_back(what, number, slot):
        x_out[number, 0] = (dka[slot] * SCALING).astype(bf16)
        x_back(what, 0).start()
        x_out[number, 1] = dva[slot].astype(bf16)
        x_back(what, 1).start()

    def far_send_back():
        x_back("pass", 0).wait_recv()
        x_out[3, 0] = (dka[3] * SCALING + x_in[2, 0].astype(f32)).astype(bf16)
        x_back("far", 0).start()
        x_back("pass", 1).wait_recv()
        x_out[3, 1] = (dva[3] + x_in[2, 1].astype(f32)).astype(bf16)
        x_back("far", 1).start()

    def at_1():
        pass_on(1)
        arrive("near")
        spread(1)

    def at_3():
        arrive("far")
        for i in range(2):
            xcopy("on", i).start()
        spread(3)

    def at_4():
        pass_on(2)
        y_arrive(3)

    def at_5():
        arrive("on")
        spread(4)

    def at_7():
        pass_on(3)

    def at_9():
        for kind in range(3):
            for way in range(2):
                ring(3, kind, way).wait_recv()

    def at_10():
        send_back(0)
        y_send_back(1)

    def at_12():
        send_back(1)
        x_send_back("near", 0, 1)
        y_arrive(1)
        y_arrive(2)

    def at_14():
        send_back(2)
        x_send_back("pass", 2, 4)

    def at_15():
        far_send_back()
        y_send_back(3)

    events = {1: at_1, 3: at_3, 4: at_4, 5: at_5, 7: at_7, 9: at_9, 10: at_10, 12: at_12, 14: at_14, 15: at_15}

    spread_loads = loads[3:]
    for load in spread_loads:
        load.wait()
    spread(0)
    arrive("sib")
    spread(2)

    def table(s, values):
        found = jnp.int32(values[0])
        for i, value in enumerate(values):
            if i > 0 and value != values[0]:
                found = jnp.where(s == i, jnp.int32(value), found)
        return found

    far_at = 32 + z * 4
    near_at = y * 8 + xh * 4
    across_at = y * 8 + (1 - xh) * 4
    one_lane = lax.broadcasted_iota(jnp.int32, (1, 128), 1)

    def step(s, carry):
        for at, event in events.items():
            pl.when(s == at)(event)
        qd = table(s, [slot for slot, _ in STEPS])
        kind = table(s, [k for _, k in STEPS])
        key_slots = [table(s, [KEY_SLOTS[k][i] for _, k in STEPS]) for i in range(2)]
        start = jnp.where(kind == FAR, far_at, jnp.where(kind == NEAR, near_at, across_at))
        own = jnp.where(kind == FAR, xl, c)
        places_of = [start + own * 2, start + (1 - own) * 2]
        shown = meta[qd, 16:17, 0:128]
        hide = {}
        for i in range(2):
            for ke in range(2):
                cells = [
                    jnp.sum(jnp.where(one_lane == places_of[i] + (e * 64 + ke), shown, 0.0), axis=1, keepdims=True)
                    for e in range(2)
                ]
                hide[i, ke] = jnp.concatenate([jnp.broadcast_to(cell, (1, 128)) for cell in cells], axis=1)
        tiles = [(i, h) for i in range(2) for h in range(HEADS)]

        def first(tile):
            i, h = tile
            cols = slice(h // 4 * 128, h // 4 * 128 + 128)
            return (
                dot(km[key_slots[i], h], qt[qd, cols, :], NN),
                dot(vm[key_slots[i], h], gt[qd, cols, :], NN),
            )

        def second(tile, scores, grad_p):
            i, h = tile
            lse, delta = meta[qd, h:h + 1, :], meta[qd, HEADS + h:HEADS + h + 1, :]
            low, grads = [], []
            for ke in range(2):
                rows = slice(ke * BLOCK, ke * BLOCK + BLOCK)
                attention = jnp.exp2(scores[rows] * (SCALING * LOG2E) - (lse + hide[i, ke]))
                low.append(attention.astype(bf16))
                grads.append((attention * (grad_p[rows] - delta)).astype(bf16))
            return jnp.concatenate(low, axis=0), jnp.concatenate(grads, axis=0)

        def third(tile, low, grads):
            i, h = tile
            rows = slice(h * HEAD_DIM, h * HEAD_DIM + HEAD_DIM)
            dva[key_slots[i], rows] += dot(gt[qd, rows, :], low, NT)
            dka[key_slots[i], rows] += dot(qt[qd, rows, :], grads, NT)
            dqa[qd, rows] += dot(kt[key_slots[i], rows, :], grads, NN)

        ones, twos = {}, {}
        for n in range(len(tiles) + 2):
            if n < len(tiles):
                ones[n] = first(tiles[n])
            if 0 <= n - 1 < len(tiles):
                twos[n - 1] = second(tiles[n - 1], *ones.pop(n - 1))
            if 0 <= n - 2 < len(tiles):
                third(tiles[n - 2], *twos.pop(n - 2))
        return carry

    lax.fori_loop(0, len(STEPS), step, 0)

    y_send_back(2)
    x_send_back("sib", 1, 2)
    send_back(3)
    for i, (out, own) in enumerate(((kg_ref, dka), (vg_ref, dva))):
        total = own[0] * SCALING if i == 0 else own[0]
        for number, what in ((0, "near"), (1, "sib"), (3, "far")):
            x_back(what, i).wait_recv()
            total = total + x_in[number, i].astype(f32)
        out[...] = total.T.astype(bf16)
    total = dqa[0] * SCALING
    for s in (1, 3, 2):
        y_back(s).wait_recv()
        total = total + y_in[s - 1].astype(f32)
    for way in range(2):
        ring_back(3, way).wait_recv()
        total = total + ring_in[3, way].astype(f32)
    qg_ref[...] = total.T.astype(bf16)

    for hop in range(4):
        for way in range(2):
            for kind in range(3):
                ring(hop, kind, way).wait_send()
            ring_back(hop, way).wait_send()
    for s in (1, 2, 3):
        for kind in range(3):
            ycopy(s, kind).wait_send()
        y_back(s).wait_send()
    for i in range(2):
        for what in ("near", "sib", "far", "on"):
            xcopy(what, i).wait_send()
        for what in ("near", "sib", "pass", "far"):
            x_back(what, i).wait_send()


def body(
    queries, key_rows, value_rows, saved_output, output_grad, log_norm,
    local_lists, expander_lists, local_counts, expander_counts,
):
    bf16, f32 = jnp.bfloat16, jnp.float32
    dma = pltpu.SemaphoreType.DMA
    tile = (ROWS, D)
    return tuple(pl.pallas_call(
        kernel,
        name="backward",
        out_shape=[jax.ShapeDtypeStruct(tile, bf16)] * 3,
        in_specs=[ANY] * 5 + [VMEM] + [SMEM] * 4,
        out_specs=[VMEM] * 3,
        scratch_shapes=[
            pltpu.VMEM(tile, bf16), pltpu.VMEM(tile, bf16), pltpu.VMEM(tile, bf16),
            pltpu.VMEM((Q_SLOTS, *tile), bf16), pltpu.VMEM((Q_SLOTS, *tile), bf16),
            pltpu.VMEM((Q_SLOTS, META, ROWS), f32),
            pltpu.VMEM((K_SLOTS, *tile), bf16), pltpu.VMEM((K_SLOTS, *tile), bf16),
            pltpu.VMEM((K_SLOTS, HEADS, ROWS, 128), bf16), pltpu.VMEM((K_SLOTS, HEADS, ROWS, 128), bf16),
            pltpu.VMEM((K_SLOTS, *tile), bf16),
            pltpu.VMEM((Q_SLOTS, *tile), f32),
            pltpu.VMEM((K_SLOTS, *tile), f32), pltpu.VMEM((K_SLOTS, *tile), f32),
            pltpu.VMEM((4, 2, *tile), bf16), pltpu.VMEM((4, 2, *tile), bf16),
            pltpu.VMEM((3, *tile), bf16), pltpu.VMEM((3, *tile), bf16),
            pltpu.VMEM((4, 2, *tile), bf16), pltpu.VMEM((4, 2, *tile), bf16),
            dma((5,)),
            dma((4, 3, 2)), dma((4, 3, 2)), dma((3, 3)), dma((3, 3)), dma((4, 2)), dma((4, 2)),
            dma((4, 2)), dma((4, 2)), dma((3,)), dma((3,)), dma((4, 2)), dma((4, 2)),
        ],
        compiler_params=pltpu.CompilerParams(
            collective_id=0, has_side_effects=True, vmem_limit_bytes=VMEM_LIMIT
        ),
    )(
        queries, output_grad, saved_output, key_rows, value_rows, log_norm,
        local_lists, expander_lists, local_counts, expander_counts,
    ))


def solution(mesh):
    rows = P(("grp", "dom"), None)
    flat = P(("grp", "dom"))
    return jax.shard_map(
        body,
        mesh=mesh,
        in_specs=(rows, rows, rows, rows, rows, P(None, ("grp", "dom")), rows, rows, flat, flat),
        out_specs=(rows, rows, rows),
        check_vma=False,
    )
```

```python
import math

import jax
import jax.numpy as jnp
from jax import lax
from jax.experimental import pallas as pl
from jax.experimental.pallas import tpu as pltpu
from jax.sharding import PartitionSpec as P

HEADS = 8
HEAD_DIM = 32
BLOCK = 128
ROWS = 256
D = 256
N_Z, N_Y = 8, 4
Q_SLOTS = 11
K_SLOTS = 5
META = 24
HIDE = 1e30
SCALING = 1.0 / math.sqrt(HEAD_DIM)
LOG2E = math.log2(math.e)
MESH = pl.DeviceIdType.MESH
ANY = pl.BlockSpec(memory_space=pl.ANY)
VMEM = pl.BlockSpec(memory_space=pltpu.VMEM)
SMEM = pl.BlockSpec(memory_space=pltpu.SMEM)
VMEM_LIMIT = 56 * 1024 * 1024
FAR, NEAR, ACROSS = 0, 1, 2
STEPS = (
    (0, NEAR), (0, FAR), (1, FAR), (7, FAR), (2, FAR), (6, FAR), (0, ACROSS), (3, FAR),
    (5, FAR), (4, FAR), (8, ACROSS), (10, ACROSS), (9, ACROSS), (9, NEAR), (8, NEAR), (10, NEAR),
)
KEY_SLOTS = {FAR: (0, 1), NEAR: (0, 2), ACROSS: (3, 4)}
NT = (((1,), (1,)), ((), ()))
NN = (((1,), (0,)), ((), ()))


def dot(a, b, dims):
    return lax.dot_general(a, b, dims, preferred_element_type=jnp.float32)


def places():
    g, m = lax.axis_index("grp"), lax.axis_index("dom")
    return g // 4, g // 2 % 2, g % 2, m // 2, m % 2


def partners(y, xh, c, z, xl):
    def at(y=y, xh=xh, c=c, z=z, xl=xl):
        return ((y * 2 + xh) * 2 + c, z * 2 + xl)

    return {
        "right": at(z=(z + 1) % N_Z),
        "left": at(z=(z + N_Z - 1) % N_Z),
        "right3": at(z=(z + 3) % N_Z),
        "left3": at(z=(z + N_Z - 3) % N_Z),
        "y1": at(y=(y + 1) % N_Y),
        "y2": at(y=(y + 2) % N_Y),
        "y3": at(y=(y + 3) % N_Y),
        "far_x": at(xh=1 - xh),
        "near_x": at(xl=1 - xl),
        "sibling": at(c=1 - c),
    }


def kernel(
    q_ref, g_ref, o_ref, k_ref, v_ref, lse_ref, ll_ref, el_ref, lc_ref, ec_ref,
    sums,
    qb, gb, ob, qt, gt, meta, kk, vv, km, vm, kt, dqa, dka, dva,
    ring_out, ring_in, y_out, y_in, x_out, x_in,
    in_sem, ring_send, ring_recv, y_send, y_recv, x_send, x_recv,
    rr_send, rr_recv, ry_send, ry_recv, rx_send, rx_recv,
):
    y, xh, c, z, xl = places()
    others = partners(y, xh, c, z, xl)
    f32, bf16 = jnp.float32, jnp.bfloat16

    def remote(src, dst, send, recv, who):
        return pltpu.make_async_remote_copy(
            src_ref=src, dst_ref=dst, send_sem=send, recv_sem=recv,
            device_id=others[who], device_id_type=MESH,
        )

    held = (qt, gt, meta)
    halves = ((0, BLOCK), (0, BLOCK), (0, 16))
    sizes = ((BLOCK, BLOCK), (BLOCK, BLOCK), (16, 8))

    def ring(hop, kind, way):
        whole = held[kind]
        src, dst = ((N_Z - hop) % N_Z, N_Z - 1 - hop) if way == 0 else (hop, hop + 1)
        src, dst = whole.at[src], whole.at[dst]
        if hop == 3:
            start = 0 if way == 0 else sizes[kind][0]
            rows = pl.ds(start, sizes[kind][way])
            src, dst = src.at[rows], dst.at[rows]
        return remote(
            src, dst, ring_send.at[hop, kind, way], ring_recv.at[hop, kind, way],
            "right" if way == 0 else "left",
        )

    def ycopy(step, kind):
        whole = held[kind]
        return remote(
            whole.at[0], whole.at[N_Z - 1 + N_Y - step], y_send.at[step - 1, kind],
            y_recv.at[step - 1, kind], f"y{step}",
        )

    def xcopy(what, i):
        whole, own = (kk, k_ref) if i == 0 else (vv, v_ref)
        number, who = {"near": (0, "near_x"), "sib": (1, "sibling"), "far": (2, "far_x"), "on": (3, "sibling")}[what]
        src = whole.at[3] if what == "on" else own
        return remote(src, whole.at[number + 1], x_send.at[number, i], x_recv.at[number, i], who)

    def ring_back(hop, way):
        buf, into = ring_out.at[hop, way], ring_in.at[hop, way]
        if hop == 0:
            rows = pl.ds(way * BLOCK, BLOCK)
            buf, into = buf.at[rows], into.at[rows]
        who = ("right", "left")[way] + ("3" if hop == 0 else "")
        return remote(buf, into, rr_send.at[hop, way], rr_recv.at[hop, way], who)

    def y_back(step):
        return remote(y_out.at[step - 1], y_in.at[step - 1], ry_send.at[step - 1], ry_recv.at[step - 1], f"y{step}")

    def x_back(what, i):
        number, who = {"near": (0, "near_x"), "sib": (1, "sibling"), "pass": (2, "sibling"), "far": (3, "far_x")}[what]
        return remote(x_out.at[number, i], x_in.at[number, i], rx_send.at[number, i], rx_recv.at[number, i], who)

    barrier = pltpu.get_barrier_semaphore()
    for device in others.values():
        pl.semaphore_signal(barrier, inc=1, device_id=device, device_id_type=MESH)
    loads = [
        pltpu.make_async_copy(src, dst, in_sem.at[i])
        for i, (src, dst) in enumerate(
            ((q_ref, qb), (g_ref, gb), (o_ref, ob), (k_ref, kk.at[0]), (v_ref, vv.at[0]))
        )
    ]
    for load in loads:
        load.start()

    lane = lax.broadcasted_iota(jnp.int32, (8, 128), 1)

    def mark(lists, counts, e, base):
        def one(s, hidden):
            hit = (lane == base + lists[e, s]) & (s < counts[e])
            return jnp.where(hit, 0.0, hidden)
        return one

    hidden = jnp.full((8, 128), HIDE, f32)
    for e in range(2):
        hidden = lax.fori_loop(0, ll_ref.shape[1], mark(ll_ref, lc_ref, e, e * 64), hidden)
        hidden = lax.fori_loop(0, el_ref.shape[1], mark(el_ref, ec_ref, e, e * 64 + 32), hidden)
    meta[0, 16:24, 0:128] = hidden
    meta[0, 16:24, 128:256] = hidden
    meta[0, 0:HEADS, :] = lse_ref[...] * LOG2E

    loads[0].wait()
    qt[0] = qb[...].astype(f32).T.astype(bf16)
    loads[1].wait()
    gt[0] = gb[...].astype(f32).T.astype(bf16)
    loads[2].wait()
    product = gb[...].astype(f32) * ob[...].astype(f32)
    high = product.astype(bf16)
    low = (product - high.astype(f32)).astype(bf16)
    rows_of = lax.broadcasted_iota(jnp.int32, (HEADS, D), 0)
    cols_of = lax.broadcasted_iota(jnp.int32, (HEADS, D), 1)
    pick = jnp.where(cols_of // HEAD_DIM == rows_of, 1.0, 0.0).astype(bf16)
    meta[0, HEADS:2 * HEADS, :] = dot(pick, high, NT) + dot(pick, low, NT)

    pl.semaphore_wait(barrier, len(others))
    for i in range(2):
        for what in ("near", "sib"):
            xcopy(what, i).start()
    for kind in range(3):
        for way in range(2):
            ring(0, kind, way).start()
        for step in (1, 3):
            ycopy(step, kind).start()
    for kind in range(3):
        ycopy(2, kind).start()

    dqa[...] = jnp.zeros_like(dqa)
    dka[...] = jnp.zeros_like(dka)
    dva[...] = jnp.zeros_like(dva)
    def spread(slot):
        kt[slot] = kk[slot].astype(f32).T.astype(bf16)
        for h in range(HEADS):
            cols = slice(h * HEAD_DIM, h * HEAD_DIM + HEAD_DIM)
            km[slot, h] = kk[slot, :, cols]
            vm[slot, h] = vv[slot, :, cols]

    def arrive(what):
        for i in range(2):
            xcopy(what, i).wait_recv()

    def pass_on(hop):
        for kind in range(3):
            for way in range(2):
                ring(hop - 1, kind, way).wait_recv()
                ring(hop, kind, way).start()

    def y_arrive(step):
        for kind in range(3):
            ycopy(step, kind).wait_recv()

    def send_back(hop, way):
        if hop == 0:
            rows = slice(way * BLOCK, way * BLOCK + BLOCK)
            ring_out[0, way, rows] = (dqa[4, rows] * SCALING).astype(bf16)
        else:
            total = dqa[4 - hop if way == 0 else 4 + hop] * SCALING
            if hop > 1:
                ring_back(hop - 1, way).wait_recv()
                total = total + ring_in[hop - 1, way].astype(f32)
            ring_out[hop, way] = total.astype(bf16)
        if hop == 3:
            rows = slice(way * BLOCK, way * BLOCK + BLOCK)
            rest = slice(BLOCK - way * BLOCK, ROWS - way * BLOCK)
            ring_back(0, way).wait_recv()
            ring_out[3, way, rows] = (total[rows] + ring_in[0, way, rows].astype(f32)).astype(bf16)
            ring_out[3, way, rest] = total[rest].astype(bf16)
        ring_back(hop, way).start()

    def y_send_back(step):
        y_out[step - 1] = (dqa[N_Z - 1 + step] * SCALING).astype(bf16)
        y_back(step).start()

    def x_send_back(what, number, slot):
        x_out[number, 0] = (dka[slot] * SCALING).astype(bf16)
        x_back(what, 0).start()
        x_out[number, 1] = dva[slot].astype(bf16)
        x_back(what, 1).start()

    def far_send_back():
        x_back("pass", 0).wait_recv()
        x_out[3, 0] = (dka[3] * SCALING + x_in[2, 0].astype(f32)).astype(bf16)
        x_back("far", 0).start()
        x_back("pass", 1).wait_recv()
        x_out[3, 1] = (dva[3] + x_in[2, 1].astype(f32)).astype(bf16)
        x_back("far", 1).start()

    def at_1():
        arrive("near")
        for i in range(2):
            xcopy("far", i).start()
        pass_on(1)
        spread(1)

    def at_4():
        pass_on(2)

    def at_5():
        arrive("far")
        for i in range(2):
            xcopy("on", i).start()
        spread(3)

    def at_6():
        arrive("on")
        spread(4)

    def at_7():
        pass_on(3)

    def at_8():
        send_back(1, 0)

    def at_9():
        send_back(1, 1)
        for kind in range(3):
            for way in range(2):
                ring(3, kind, way).wait_recv()

    def at_10():
        send_back(0, 0)
        send_back(0, 1)
        x_send_back("near", 0, 1)
        for step in (1, 2, 3):
            y_arrive(step)

    def at_11():
        send_back(2, 0)

    def at_12():
        send_back(2, 1)

    def at_13():
        x_send_back("pass", 2, 4)

    def at_14():
        far_send_back()
        send_back(3, 0)
        y_send_back(2)

    def at_15():
        send_back(3, 1)
        y_send_back(1)

    events = {
        1: at_1, 4: at_4, 5: at_5, 6: at_6, 7: at_7, 8: at_8, 9: at_9, 10: at_10, 11: at_11, 12: at_12,
        13: at_13, 14: at_14, 15: at_15,
    }

    spread_loads = loads[3:]
    for load in spread_loads:
        load.wait()
    spread(0)
    arrive("sib")
    spread(2)

    def table(s, values):
        found = jnp.int32(values[0])
        for i, value in enumerate(values):
            if i > 0 and value != values[0]:
                found = jnp.where(s == i, jnp.int32(value), found)
        return found

    far_at = 32 + z * 4
    near_at = y * 8 + xh * 4
    across_at = y * 8 + (1 - xh) * 4
    one_lane = lax.broadcasted_iota(jnp.int32, (1, 128), 1)

    def step(s, carry):
        for at, event in events.items():
            pl.when(s == at)(event)
        qd = table(s, [slot for slot, _ in STEPS])
        kind = table(s, [k for _, k in STEPS])
        key_slots = [table(s, [KEY_SLOTS[k][i] for _, k in STEPS]) for i in range(2)]
        start = jnp.where(kind == FAR, far_at, jnp.where(kind == NEAR, near_at, across_at))
        own = jnp.where(kind == FAR, xl, c)
        places_of = [start + own * 2, start + (1 - own) * 2]
        shown = meta[qd, 16:17, 0:128]
        hide = {}
        for i in range(2):
            for ke in range(2):
                cells = [
                    jnp.sum(jnp.where(one_lane == places_of[i] + (e * 64 + ke), shown, 0.0), axis=1, keepdims=True)
                    for e in range(2)
                ]
                hide[i, ke] = jnp.concatenate([jnp.broadcast_to(cell, (1, 128)) for cell in cells], axis=1)
        tiles = [(i, h) for i in range(2) for h in range(HEADS)]

        def first(tile):
            i, h = tile
            rows = slice(h * HEAD_DIM, h * HEAD_DIM + HEAD_DIM)
            return (
                dot(km[key_slots[i], h], qt[qd, rows, :], NN),
                dot(vm[key_slots[i], h], gt[qd, rows, :], NN),
            )

        def second(tile, scores, grad_p):
            i, h = tile
            lse, delta = meta[qd, h:h + 1, :], meta[qd, HEADS + h:HEADS + h + 1, :]
            low, grads = [], []
            for ke in range(2):
                rows = slice(ke * BLOCK, ke * BLOCK + BLOCK)
                attention = jnp.exp2(scores[rows] * (SCALING * LOG2E) - (lse + hide[i, ke]))
                low.append(attention.astype(bf16))
                grads.append((attention * (grad_p[rows] - delta)).astype(bf16))
            return jnp.concatenate(low, axis=0), jnp.concatenate(grads, axis=0)

        def third(tile, low, grads):
            i, h = tile
            rows = slice(h * HEAD_DIM, h * HEAD_DIM + HEAD_DIM)
            dva[key_slots[i], rows] += dot(gt[qd, rows, :], low, NT)
            dka[key_slots[i], rows] += dot(qt[qd, rows, :], grads, NT)
            dqa[qd, rows] += dot(kt[key_slots[i], rows, :], grads, NN)

        ones, twos = {}, {}
        for n in range(len(tiles) + 2):
            if n < len(tiles):
                ones[n] = first(tiles[n])
            if 0 <= n - 1 < len(tiles):
                twos[n - 1] = second(tiles[n - 1], *ones.pop(n - 1))
            if 0 <= n - 2 < len(tiles):
                third(tiles[n - 2], *twos.pop(n - 2))
        return carry

    lax.fori_loop(0, len(STEPS), step, 0)

    y_send_back(3)
    x_send_back("sib", 1, 2)
    for i, own in enumerate((dka, dva)):
        total = own[0] * SCALING if i == 0 else own[0]
        for number, what in ((0, "near"), (1, "sib"), (3, "far")):
            x_back(what, i).wait_recv()
            total = total + x_in[number, i].astype(f32)
        sums[1 + i] = total.astype(bf16)
    total = dqa[0] * SCALING
    for s in (2, 1, 3):
        y_back(s).wait_recv()
        total = total + y_in[s - 1].astype(f32)
    for way in range(2):
        ring_back(3, way).wait_recv()
        total = total + ring_in[3, way].astype(f32)
    sums[0] = total.astype(bf16)

    for hop in range(4):
        for way in range(2):
            for kind in range(3):
                ring(hop, kind, way).wait_send()
            ring_back(hop, way).wait_send()
    for s in (1, 2, 3):
        for kind in range(3):
            ycopy(s, kind).wait_send()
        y_back(s).wait_send()
    for i in range(2):
        for what in ("near", "sib", "far", "on"):
            xcopy(what, i).wait_send()
        for what in ("near", "sib", "pass", "far"):
            x_back(what, i).wait_send()


def turn_kernel(sums, *outs):
    for i, out in enumerate(outs):
        out[...] = sums[i].astype(jnp.float32).T.astype(jnp.bfloat16)


def body(
    queries, key_rows, value_rows, saved_output, output_grad, log_norm,
    local_lists, expander_lists, local_counts, expander_counts,
):
    bf16, f32 = jnp.bfloat16, jnp.float32
    dma = pltpu.SemaphoreType.DMA
    tile = (ROWS, D)
    sums = pl.pallas_call(
        kernel,
        name="backward",
        out_shape=jax.ShapeDtypeStruct((3, *tile), bf16),
        in_specs=[ANY] * 5 + [VMEM] + [SMEM] * 4,
        out_specs=VMEM,
        scratch_shapes=[
            pltpu.VMEM(tile, bf16), pltpu.VMEM(tile, bf16), pltpu.VMEM(tile, bf16),
            pltpu.VMEM((Q_SLOTS, *tile), bf16), pltpu.VMEM((Q_SLOTS, *tile), bf16),
            pltpu.VMEM((Q_SLOTS, META, ROWS), f32),
            pltpu.VMEM((K_SLOTS, *tile), bf16), pltpu.VMEM((K_SLOTS, *tile), bf16),
            pltpu.VMEM((K_SLOTS, HEADS, ROWS, HEAD_DIM), bf16), pltpu.VMEM((K_SLOTS, HEADS, ROWS, HEAD_DIM), bf16),
            pltpu.VMEM((K_SLOTS, *tile), bf16),
            pltpu.VMEM((Q_SLOTS, *tile), f32),
            pltpu.VMEM((K_SLOTS, *tile), f32), pltpu.VMEM((K_SLOTS, *tile), f32),
            pltpu.VMEM((4, 2, *tile), bf16), pltpu.VMEM((4, 2, *tile), bf16),
            pltpu.VMEM((3, *tile), bf16), pltpu.VMEM((3, *tile), bf16),
            pltpu.VMEM((4, 2, *tile), bf16), pltpu.VMEM((4, 2, *tile), bf16),
            dma((5,)),
            dma((4, 3, 2)), dma((4, 3, 2)), dma((3, 3)), dma((3, 3)), dma((4, 2)), dma((4, 2)),
            dma((4, 2)), dma((4, 2)), dma((3,)), dma((3,)), dma((4, 2)), dma((4, 2)),
        ],
        compiler_params=pltpu.CompilerParams(
            collective_id=0, has_side_effects=True, vmem_limit_bytes=VMEM_LIMIT
        ),
    )(
        queries, output_grad, saved_output, key_rows, value_rows, log_norm,
        local_lists, expander_lists, local_counts, expander_counts,
    )
    return tuple(pl.pallas_call(
        turn_kernel,
        name="turn",
        out_shape=[jax.ShapeDtypeStruct(tile, bf16)] * 3,
        in_specs=[VMEM],
        out_specs=[VMEM] * 3,
    )(sums))


def solution(mesh):
    rows = P(("grp", "dom"), None)
    flat = P(("grp", "dom"))
    return jax.shard_map(
        body,
        mesh=mesh,
        in_specs=(rows, rows, rows, rows, rows, P(None, ("grp", "dom")), rows, rows, flat, flat),
        out_specs=(rows, rows, rows),
        check_vma=False,
    )
```

```python
import math

import jax
import jax.numpy as jnp
from jax import lax
from jax.experimental import pallas as pl
from jax.experimental.pallas import tpu as pltpu
from jax.sharding import PartitionSpec as P

HEADS = 8
HEAD_DIM = 32
BLOCK = 128
ROWS = 256
D = 256
N_Z, N_Y = 8, 4
Q_SLOTS = 11
K_SLOTS = 5
META = 24
HIDE = 1e30
SCALING = 1.0 / math.sqrt(HEAD_DIM)
LOG2E = math.log2(math.e)
MESH = pl.DeviceIdType.MESH
ANY = pl.BlockSpec(memory_space=pl.ANY)
VMEM = pl.BlockSpec(memory_space=pltpu.VMEM)
SMEM = pl.BlockSpec(memory_space=pltpu.SMEM)
VMEM_LIMIT = 56 * 1024 * 1024
FAR, NEAR, ACROSS = 0, 1, 2
STEPS = (
    (0, NEAR), (0, FAR), (1, FAR), (7, FAR), (2, FAR), (6, FAR), (0, ACROSS), (8, ACROSS),
    (10, ACROSS), (3, FAR), (5, FAR), (4, FAR), (9, ACROSS), (9, NEAR), (8, NEAR), (10, NEAR),
)
KEY_SLOTS = {FAR: (0, 1), NEAR: (0, 2), ACROSS: (3, 4)}
NT = (((1,), (1,)), ((), ()))
NN = (((1,), (0,)), ((), ()))


def dot(a, b, dims):
    return lax.dot_general(a, b, dims, preferred_element_type=jnp.float32)


def places():
    g, m = lax.axis_index("grp"), lax.axis_index("dom")
    return g // 4, g // 2 % 2, g % 2, m // 2, m % 2


def partners(y, xh, c, z, xl):
    def at(y=y, xh=xh, c=c, z=z, xl=xl):
        return ((y * 2 + xh) * 2 + c, z * 2 + xl)

    return {
        "right": at(z=(z + 1) % N_Z),
        "left": at(z=(z + N_Z - 1) % N_Z),
        "right3": at(z=(z + 3) % N_Z),
        "left3": at(z=(z + N_Z - 3) % N_Z),
        "y1": at(y=(y + 1) % N_Y),
        "y2": at(y=(y + 2) % N_Y),
        "y3": at(y=(y + 3) % N_Y),
        "far_x": at(xh=1 - xh),
        "near_x": at(xl=1 - xl),
        "sibling": at(c=1 - c),
    }


def kernel(
    q_ref, g_ref, o_ref, k_ref, v_ref, lse_ref, ll_ref, el_ref, lc_ref, ec_ref,
    sums,
    qb, gb, ob, qt, gt, meta, kk, vv, km, vm, kt, dqa, dka, dva,
    ring_out, ring_in, y_out, y_in, x_out, x_in,
    in_sem, ring_send, ring_recv, y_send, y_recv, x_send, x_recv,
    rr_send, rr_recv, ry_send, ry_recv, rx_send, rx_recv,
):
    y, xh, c, z, xl = places()
    others = partners(y, xh, c, z, xl)
    f32, bf16 = jnp.float32, jnp.bfloat16

    def remote(src, dst, send, recv, who):
        return pltpu.make_async_remote_copy(
            src_ref=src, dst_ref=dst, send_sem=send, recv_sem=recv,
            device_id=others[who], device_id_type=MESH,
        )

    held = (qt, gt, meta)
    halves = ((0, BLOCK), (0, BLOCK), (0, 16))
    sizes = ((BLOCK, BLOCK), (BLOCK, BLOCK), (16, 8))

    def ring(hop, kind, way):
        whole = held[kind]
        src, dst = ((N_Z - hop) % N_Z, N_Z - 1 - hop) if way == 0 else (hop, hop + 1)
        src, dst = whole.at[src], whole.at[dst]
        if hop == 3:
            start = 0 if way == 0 else sizes[kind][0]
            rows = pl.ds(start, sizes[kind][way])
            src, dst = src.at[rows], dst.at[rows]
        return remote(
            src, dst, ring_send.at[hop, kind, way], ring_recv.at[hop, kind, way],
            "right" if way == 0 else "left",
        )

    def ycopy(step, kind):
        whole = held[kind]
        return remote(
            whole.at[0], whole.at[N_Z - 1 + N_Y - step], y_send.at[step - 1, kind],
            y_recv.at[step - 1, kind], f"y{step}",
        )

    def xcopy(what, i):
        whole, own = (kk, k_ref) if i == 0 else (vv, v_ref)
        number, who = {"near": (0, "near_x"), "sib": (1, "sibling"), "far": (2, "far_x"), "on": (3, "sibling")}[what]
        src = whole.at[3] if what == "on" else own
        return remote(src, whole.at[number + 1], x_send.at[number, i], x_recv.at[number, i], who)

    def ring_back(hop, way):
        buf, into = ring_out.at[hop, way], ring_in.at[hop, way]
        if hop == 0:
            rows = pl.ds(way * BLOCK, BLOCK)
            buf, into = buf.at[rows], into.at[rows]
        who = ("right", "left")[way] + ("3" if hop == 0 else "")
        return remote(buf, into, rr_send.at[hop, way], rr_recv.at[hop, way], who)

    def y_back(step, half=None):
        buf, into = y_out.at[step - 1], y_in.at[step - 1]
        if half is not None:
            rows = pl.ds(half * BLOCK, BLOCK)
            buf, into = buf.at[rows], into.at[rows]
        at = (step - 1, half or 0)
        return remote(buf, into, ry_send.at[at], ry_recv.at[at], f"y{step}")

    def x_back(what, i):
        number, who = {"near": (0, "near_x"), "sib": (1, "sibling"), "pass": (2, "sibling"), "far": (3, "far_x")}[what]
        return remote(x_out.at[number, i], x_in.at[number, i], rx_send.at[number, i], rx_recv.at[number, i], who)

    barrier = pltpu.get_barrier_semaphore()
    for device in others.values():
        pl.semaphore_signal(barrier, inc=1, device_id=device, device_id_type=MESH)
    loads = [
        pltpu.make_async_copy(src, dst, in_sem.at[i])
        for i, (src, dst) in enumerate(
            ((q_ref, qb), (g_ref, gb), (o_ref, ob), (k_ref, kk.at[0]), (v_ref, vv.at[0]))
        )
    ]
    for load in loads:
        load.start()

    lane = lax.broadcasted_iota(jnp.int32, (8, 128), 1)

    def mark(lists, counts, e, base):
        def one(s, hidden):
            hit = (lane == base + lists[e, s]) & (s < counts[e])
            return jnp.where(hit, 0.0, hidden)
        return one

    hidden = jnp.full((8, 128), HIDE, f32)
    for e in range(2):
        hidden = lax.fori_loop(0, ll_ref.shape[1], mark(ll_ref, lc_ref, e, e * 64), hidden)
        hidden = lax.fori_loop(0, el_ref.shape[1], mark(el_ref, ec_ref, e, e * 64 + 32), hidden)
    meta[0, 16:24, 0:128] = hidden
    meta[0, 16:24, 128:256] = hidden
    meta[0, 0:HEADS, :] = lse_ref[...] * LOG2E

    loads[0].wait()
    qt[0] = qb[...].astype(f32).T.astype(bf16)
    loads[1].wait()
    gt[0] = gb[...].astype(f32).T.astype(bf16)
    loads[2].wait()
    product = gb[...].astype(f32) * ob[...].astype(f32)
    high = product.astype(bf16)
    low = (product - high.astype(f32)).astype(bf16)
    rows_of = lax.broadcasted_iota(jnp.int32, (HEADS, D), 0)
    cols_of = lax.broadcasted_iota(jnp.int32, (HEADS, D), 1)
    pick = jnp.where(cols_of // HEAD_DIM == rows_of, 1.0, 0.0).astype(bf16)
    meta[0, HEADS:2 * HEADS, :] = dot(pick, high, NT) + dot(pick, low, NT)

    pl.semaphore_wait(barrier, len(others))
    for i in range(2):
        for what in ("near", "sib"):
            xcopy(what, i).start()
    for kind in range(3):
        for way in range(2):
            ring(0, kind, way).start()
        for step in (1, 3):
            ycopy(step, kind).start()
    for kind in range(3):
        ycopy(2, kind).start()

    dqa[...] = jnp.zeros_like(dqa)
    dka[...] = jnp.zeros_like(dka)
    dva[...] = jnp.zeros_like(dva)
    def spread(slot):
        kt[slot] = kk[slot].astype(f32).T.astype(bf16)
        for h in range(HEADS):
            cols = slice(h * HEAD_DIM, h * HEAD_DIM + HEAD_DIM)
            km[slot, h] = kk[slot, :, cols]
            vm[slot, h] = vv[slot, :, cols]

    def arrive(what):
        for i in range(2):
            xcopy(what, i).wait_recv()

    def pass_on(hop):
        for kind in range(3):
            for way in range(2):
                ring(hop - 1, kind, way).wait_recv()
                ring(hop, kind, way).start()

    def y_arrive(step):
        for kind in range(3):
            ycopy(step, kind).wait_recv()

    def send_back(hop, way):
        if hop == 0:
            rows = slice(way * BLOCK, way * BLOCK + BLOCK)
            ring_out[0, way, rows] = (dqa[4, rows] * SCALING).astype(bf16)
        else:
            total = dqa[4 - hop if way == 0 else 4 + hop] * SCALING
            if hop > 1:
                ring_back(hop - 1, way).wait_recv()
                total = total + ring_in[hop - 1, way].astype(f32)
            ring_out[hop, way] = total.astype(bf16)
        if hop == 3:
            rows = slice(way * BLOCK, way * BLOCK + BLOCK)
            rest = slice(BLOCK - way * BLOCK, ROWS - way * BLOCK)
            ring_back(0, way).wait_recv()
            ring_out[3, way, rows] = (total[rows] + ring_in[0, way, rows].astype(f32)).astype(bf16)
            ring_out[3, way, rest] = total[rest].astype(bf16)
        ring_back(hop, way).start()

    def y_send_back(step, half=None):
        rows = slice(None) if half is None else slice(half * BLOCK, half * BLOCK + BLOCK)
        y_out[step - 1, rows] = (dqa[N_Z - 1 + step, rows] * SCALING).astype(bf16)
        y_back(step, half).start()

    def x_send_back(what, number, slot):
        x_out[number, 0] = (dka[slot] * SCALING).astype(bf16)
        x_back(what, 0).start()
        x_out[number, 1] = dva[slot].astype(bf16)
        x_back(what, 1).start()

    def far_send_back():
        x_back("pass", 0).wait_recv()
        x_out[3, 0] = (dka[3] * SCALING + x_in[2, 0].astype(f32)).astype(bf16)
        x_back("far", 0).start()
        x_back("pass", 1).wait_recv()
        x_out[3, 1] = (dva[3] + x_in[2, 1].astype(f32)).astype(bf16)
        x_back("far", 1).start()

    def at_1():
        arrive("near")
        for i in range(2):
            xcopy("far", i).start()
        pass_on(1)
        spread(1)

    def at_4():
        pass_on(2)

    def at_5():
        arrive("far")
        for i in range(2):
            xcopy("on", i).start()
        spread(3)

    def at_6():
        arrive("on")
        spread(4)

    def at_7():
        y_arrive(3)

    def at_8():
        pass_on(3)
        y_arrive(1)

    def at_10():
        send_back(1, 0)

    def at_11():
        send_back(1, 1)
        for kind in range(3):
            for way in range(2):
                ring(3, kind, way).wait_recv()

    def at_12():
        x_send_back("near", 0, 1)
        send_back(0, 0)
        send_back(0, 1)
        y_arrive(2)

    def at_13():
        x_send_back("pass", 2, 4)
        send_back(2, 0)
        send_back(2, 1)

    def at_14():
        far_send_back()
        y_send_back(2)

    def at_15():
        y_send_back(1)
        send_back(3, 0)
        send_back(3, 1)

    events = {
        1: at_1, 4: at_4, 5: at_5, 6: at_6, 7: at_7, 8: at_8, 10: at_10, 11: at_11, 12: at_12,
        13: at_13, 14: at_14, 15: at_15,
    }

    spread_loads = loads[3:]
    for load in spread_loads:
        load.wait()
    spread(0)
    arrive("sib")
    spread(2)

    def table(s, values):
        if isinstance(s, int):
            return values[s]
        found = jnp.int32(values[0])
        for i, value in enumerate(values):
            if i > 0 and value != values[0]:
                found = jnp.where(s == i, jnp.int32(value), found)
        return found

    far_at = 32 + z * 4
    near_at = y * 8 + xh * 4
    across_at = y * 8 + (1 - xh) * 4
    one_lane = lax.broadcasted_iota(jnp.int32, (1, 128), 1)

    def step(s, carry):
        last = isinstance(s, int)
        for at, event in events.items():
            if not last:
                pl.when(s == at)(event)
            elif s == at:
                event()
        qd = table(s, [slot for slot, _ in STEPS])
        kind = table(s, [k for _, k in STEPS])
        key_slots = [table(s, [KEY_SLOTS[k][i] for _, k in STEPS]) for i in range(2)]
        start = near_at if last else jnp.where(kind == FAR, far_at, jnp.where(kind == NEAR, near_at, across_at))
        own = c if last else jnp.where(kind == FAR, xl, c)
        places_of = [start + own * 2, start + (1 - own) * 2]
        shown = meta[qd, 16:17, 0:128]
        hide = {}
        for i in range(2):
            for ke in range(2):
                cells = [
                    jnp.sum(jnp.where(one_lane == places_of[i] + (e * 64 + ke), shown, 0.0), axis=1, keepdims=True)
                    for e in range(2)
                ]
                hide[i, ke] = jnp.concatenate([jnp.broadcast_to(cell, (1, 128)) for cell in cells], axis=1)
        tiles = [(i, h) for h in range(HEADS) for i in range(2)]

        def first(tile):
            i, h = tile
            rows = slice(h * HEAD_DIM, h * HEAD_DIM + HEAD_DIM)
            return (
                dot(km[key_slots[i], h], qt[qd, rows, :], NN),
                dot(vm[key_slots[i], h], gt[qd, rows, :], NN),
            )

        def second(tile, scores, grad_p):
            i, h = tile
            lse, delta = meta[qd, h:h + 1, :], meta[qd, HEADS + h:HEADS + h + 1, :]
            low, grads = [], []
            for ke in range(2):
                rows = slice(ke * BLOCK, ke * BLOCK + BLOCK)
                attention = jnp.exp2(scores[rows] * (SCALING * LOG2E) - (lse + hide[i, ke]))
                low.append(attention.astype(bf16))
                grads.append((attention * (grad_p[rows] - delta)).astype(bf16))
            return jnp.concatenate(low, axis=0), jnp.concatenate(grads, axis=0)

        def third(tile, low, grads):
            i, h = tile
            rows = slice(h * HEAD_DIM, h * HEAD_DIM + HEAD_DIM)
            dva[key_slots[i], rows] += dot(gt[qd, rows, :], low, NT)
            dka[key_slots[i], rows] += dot(qt[qd, rows, :], grads, NT)
            dqa[qd, rows] += dot(kt[key_slots[i], rows, :], grads, NN)

        ones, twos = {}, {}
        for n in range(len(tiles) + 2):
            if n < len(tiles):
                ones[n] = first(tiles[n])
            if 0 <= n - 1 < len(tiles):
                twos[n - 1] = second(tiles[n - 1], *ones.pop(n - 1))
            if 0 <= n - 2 < len(tiles):
                third(tiles[n - 2], *twos.pop(n - 2))
            if last and n - 2 == len(tiles) // 2 - 1:
                y_send_back(3, 0)
        return carry

    lax.fori_loop(0, len(STEPS) - 1, step, 0)
    step(len(STEPS) - 1, 0)

    y_send_back(3, 1)
    x_send_back("sib", 1, 2)
    for i, own in enumerate((dka, dva)):
        total = own[0] * SCALING if i == 0 else own[0]
        for number, what in ((0, "near"), (1, "sib"), (3, "far")):
            x_back(what, i).wait_recv()
            total = total + x_in[number, i].astype(f32)
        sums[1 + i] = total.T.astype(bf16)
    total = dqa[0] * SCALING
    y_back(2).wait_recv()
    y_back(1).wait_recv()
    total = total + y_in[0].astype(f32) + y_in[1].astype(f32)
    for way in range(2):
        ring_back(3, way).wait_recv()
        total = total + ring_in[3, way].astype(f32)
    for half in range(2):
        y_back(3, half).wait_recv()
    total = total + y_in[2].astype(f32)
    sums[0] = total.astype(bf16)

    for hop in range(4):
        for way in range(2):
            for kind in range(3):
                ring(hop, kind, way).wait_send()
            ring_back(hop, way).wait_send()
    for s in (1, 2, 3):
        for kind in range(3):
            ycopy(s, kind).wait_send()
    y_back(1).wait_send()
    y_back(2).wait_send()
    for half in range(2):
        y_back(3, half).wait_send()
    for i in range(2):
        for what in ("near", "sib", "far", "on"):
            xcopy(what, i).wait_send()
        for what in ("near", "sib", "pass", "far"):
            x_back(what, i).wait_send()


def turn_kernel(sums, q_out, k_out, v_out):
    q_out[...] = sums[0].astype(jnp.float32).T.astype(jnp.bfloat16)
    k_out[...] = sums[1]
    v_out[...] = sums[2]


def body(
    queries, key_rows, value_rows, saved_output, output_grad, log_norm,
    local_lists, expander_lists, local_counts, expander_counts,
):
    bf16, f32 = jnp.bfloat16, jnp.float32
    dma = pltpu.SemaphoreType.DMA
    tile = (ROWS, D)
    sums = pl.pallas_call(
        kernel,
        name="backward",
        out_shape=jax.ShapeDtypeStruct((3, *tile), bf16),
        in_specs=[ANY] * 5 + [VMEM] + [SMEM] * 4,
        out_specs=VMEM,
        scratch_shapes=[
            pltpu.VMEM(tile, bf16), pltpu.VMEM(tile, bf16), pltpu.VMEM(tile, bf16),
            pltpu.VMEM((Q_SLOTS, *tile), bf16), pltpu.VMEM((Q_SLOTS, *tile), bf16),
            pltpu.VMEM((Q_SLOTS, META, ROWS), f32),
            pltpu.VMEM((K_SLOTS, *tile), bf16), pltpu.VMEM((K_SLOTS, *tile), bf16),
            pltpu.VMEM((K_SLOTS, HEADS, ROWS, HEAD_DIM), bf16), pltpu.VMEM((K_SLOTS, HEADS, ROWS, HEAD_DIM), bf16),
            pltpu.VMEM((K_SLOTS, *tile), bf16),
            pltpu.VMEM((Q_SLOTS, *tile), f32),
            pltpu.VMEM((K_SLOTS, *tile), f32), pltpu.VMEM((K_SLOTS, *tile), f32),
            pltpu.VMEM((4, 2, *tile), bf16), pltpu.VMEM((4, 2, *tile), bf16),
            pltpu.VMEM((3, *tile), bf16), pltpu.VMEM((3, *tile), bf16),
            pltpu.VMEM((4, 2, *tile), bf16), pltpu.VMEM((4, 2, *tile), bf16),
            dma((5,)),
            dma((4, 3, 2)), dma((4, 3, 2)), dma((3, 3)), dma((3, 3)), dma((4, 2)), dma((4, 2)),
            dma((4, 2)), dma((4, 2)), dma((3, 2)), dma((3, 2)), dma((4, 2)), dma((4, 2)),
        ],
        compiler_params=pltpu.CompilerParams(
            collective_id=0, has_side_effects=True, vmem_limit_bytes=VMEM_LIMIT
        ),
    )(
        queries, output_grad, saved_output, key_rows, value_rows, log_norm,
        local_lists, expander_lists, local_counts, expander_counts,
    )
    return tuple(pl.pallas_call(
        turn_kernel,
        name="turn",
        out_shape=[jax.ShapeDtypeStruct(tile, bf16)] * 3,
        in_specs=[VMEM],
        out_specs=[VMEM] * 3,
    )(sums))


def solution(mesh):
    rows = P(("grp", "dom"), None)
    flat = P(("grp", "dom"))
    return jax.shard_map(
        body,
        mesh=mesh,
        in_specs=(rows, rows, rows, rows, rows, P(None, ("grp", "dom")), rows, rows, flat, flat),
        out_specs=(rows, rows, rows),
        check_vma=False,
    )
```

```python
import math

import jax
import jax.numpy as jnp
from jax import lax
from jax.experimental import pallas as pl
from jax.experimental.pallas import tpu as pltpu
from jax.sharding import PartitionSpec as P

HEADS = 8
HEAD_DIM = 32
BLOCK = 128
ROWS = 256
D = 256
N_Z, N_Y = 8, 4
Q_SLOTS = 11
K_SLOTS = 5
META = 24
HIDE = 1e30
SCALING = 1.0 / math.sqrt(HEAD_DIM)
LOG2E = math.log2(math.e)
MESH = pl.DeviceIdType.MESH
ANY = pl.BlockSpec(memory_space=pl.ANY)
VMEM = pl.BlockSpec(memory_space=pltpu.VMEM)
SMEM = pl.BlockSpec(memory_space=pltpu.SMEM)
VMEM_LIMIT = 56 * 1024 * 1024
FAR, NEAR, ACROSS = 0, 1, 2
STEPS = (
    (0, NEAR), (0, FAR), (1, FAR), (7, FAR), (2, FAR), (6, FAR), (0, ACROSS), (8, ACROSS),
    (10, ACROSS), (3, FAR), (5, FAR), (4, FAR), (9, ACROSS), (9, NEAR), (8, NEAR), (10, NEAR),
)
KEY_SLOTS = {FAR: (0, 1), NEAR: (0, 2), ACROSS: (3, 4)}
NT = (((1,), (1,)), ((), ()))
NN = (((1,), (0,)), ((), ()))


def dot(a, b, dims):
    return lax.dot_general(a, b, dims, preferred_element_type=jnp.float32)


def places():
    g, m = lax.axis_index("grp"), lax.axis_index("dom")
    return g // 4, g // 2 % 2, g % 2, m // 2, m % 2


def partners(y, xh, c, z, xl):
    def at(y=y, xh=xh, c=c, z=z, xl=xl):
        return ((y * 2 + xh) * 2 + c, z * 2 + xl)

    return {
        "right": at(z=(z + 1) % N_Z),
        "left": at(z=(z + N_Z - 1) % N_Z),
        "right3": at(z=(z + 3) % N_Z),
        "left3": at(z=(z + N_Z - 3) % N_Z),
        "y1": at(y=(y + 1) % N_Y),
        "y2": at(y=(y + 2) % N_Y),
        "y3": at(y=(y + 3) % N_Y),
        "far_x": at(xh=1 - xh),
        "near_x": at(xl=1 - xl),
        "sibling": at(c=1 - c),
    }


def kernel(
    q_ref, g_ref, o_ref, k_ref, v_ref, lse_hbm, ll_hbm, el_hbm, lc_ref, ec_ref,
    sums,
    lse_ref, ll_ref, el_ref,
    qb, gb, ob, qt, gt, meta, kk, vv, km, vm, kt, dqa, dka, dva,
    ring_out, ring_in, y_out, y_in, x_out, x_in,
    in_sem, ring_send, ring_recv, y_send, y_recv, x_send, x_recv,
    rr_send, rr_recv, ry_send, ry_recv, rx_send, rx_recv,
):
    y, xh, c, z, xl = places()
    others = partners(y, xh, c, z, xl)
    f32, bf16 = jnp.float32, jnp.bfloat16

    def remote(src, dst, send, recv, who):
        return pltpu.make_async_remote_copy(
            src_ref=src, dst_ref=dst, send_sem=send, recv_sem=recv,
            device_id=others[who], device_id_type=MESH,
        )

    held = (qt, gt, meta)
    halves = ((0, BLOCK), (0, BLOCK), (0, 16))
    sizes = ((BLOCK, BLOCK), (BLOCK, BLOCK), (16, 8))

    def ring(hop, kind, way):
        whole = held[kind]
        src, dst = ((N_Z - hop) % N_Z, N_Z - 1 - hop) if way == 0 else (hop, hop + 1)
        src, dst = whole.at[src], whole.at[dst]
        if hop == 3:
            start = 0 if way == 0 else sizes[kind][0]
            rows = pl.ds(start, sizes[kind][way])
            src, dst = src.at[rows], dst.at[rows]
        return remote(
            src, dst, ring_send.at[hop, kind, way], ring_recv.at[hop, kind, way],
            "right" if way == 0 else "left",
        )

    def ycopy(step, kind):
        whole = held[kind]
        return remote(
            whole.at[0], whole.at[N_Z - 1 + N_Y - step], y_send.at[step - 1, kind],
            y_recv.at[step - 1, kind], f"y{step}",
        )

    def xcopy(what, i):
        whole, own = (kk, k_ref) if i == 0 else (vv, v_ref)
        number, who = {"near": (0, "near_x"), "sib": (1, "sibling"), "far": (2, "far_x"), "on": (3, "sibling")}[what]
        src = whole.at[3] if what == "on" else own
        return remote(src, whole.at[number + 1], x_send.at[number, i], x_recv.at[number, i], who)

    def ring_back(hop, way):
        buf, into = ring_out.at[hop, way], ring_in.at[hop, way]
        if hop == 0:
            rows = pl.ds(way * BLOCK, BLOCK)
            buf, into = buf.at[rows], into.at[rows]
        who = ("right", "left")[way] + ("3" if hop == 0 else "")
        return remote(buf, into, rr_send.at[hop, way], rr_recv.at[hop, way], who)

    def y_back(step, half=None):
        buf, into = y_out.at[step - 1], y_in.at[step - 1]
        if half is not None:
            rows = pl.ds(half * BLOCK, BLOCK)
            buf, into = buf.at[rows], into.at[rows]
        at = (step - 1, half or 0)
        return remote(buf, into, ry_send.at[at], ry_recv.at[at], f"y{step}")

    def x_back(what, i):
        number, who = {"near": (0, "near_x"), "sib": (1, "sibling"), "pass": (2, "sibling"), "far": (3, "far_x")}[what]
        return remote(x_out.at[number, i], x_in.at[number, i], rx_send.at[number, i], rx_recv.at[number, i], who)

    barrier = pltpu.get_barrier_semaphore()
    for device in others.values():
        pl.semaphore_signal(barrier, inc=1, device_id=device, device_id_type=MESH)
    loads = [
        pltpu.make_async_copy(src, dst, in_sem.at[i])
        for i, (src, dst) in enumerate(
            (
                (q_ref, qb), (g_ref, gb), (o_ref, ob), (k_ref, kk.at[0]), (v_ref, vv.at[0]),
                (lse_hbm, lse_ref), (ll_hbm, ll_ref), (el_hbm, el_ref),
            )
        )
    ]
    for load in loads:
        load.start()

    lane = lax.broadcasted_iota(jnp.int32, (8, 128), 1)

    def mark(lists, counts, e, base):
        def one(s, hidden):
            hit = (lane == base + lists[e, s]) & (s < counts[e])
            return jnp.where(hit, 0.0, hidden)
        return one

    for load in loads[5:]:
        load.wait()
    hidden = jnp.full((8, 128), HIDE, f32)
    for e in range(2):
        hidden = lax.fori_loop(0, ll_ref.shape[1], mark(ll_ref, lc_ref, e, e * 64), hidden)
        hidden = lax.fori_loop(0, el_ref.shape[1], mark(el_ref, ec_ref, e, e * 64 + 32), hidden)
    meta[0, 16:24, 0:128] = hidden
    meta[0, 16:24, 128:256] = hidden
    meta[0, 0:HEADS, :] = lse_ref[...] * LOG2E

    loads[0].wait()
    qt[0] = qb[...].astype(f32).T.astype(bf16)
    loads[1].wait()
    gt[0] = gb[...].astype(f32).T.astype(bf16)
    loads[2].wait()
    product = gb[...].astype(f32) * ob[...].astype(f32)
    high = product.astype(bf16)
    low = (product - high.astype(f32)).astype(bf16)
    rows_of = lax.broadcasted_iota(jnp.int32, (HEADS, D), 0)
    cols_of = lax.broadcasted_iota(jnp.int32, (HEADS, D), 1)
    pick = jnp.where(cols_of // HEAD_DIM == rows_of, 1.0, 0.0).astype(bf16)
    meta[0, HEADS:2 * HEADS, :] = dot(pick, high, NT) + dot(pick, low, NT)

    pl.semaphore_wait(barrier, len(others))
    for i in range(2):
        for what in ("near", "sib"):
            xcopy(what, i).start()
    for kind in range(3):
        for way in range(2):
            ring(0, kind, way).start()
        for step in (1, 3):
            ycopy(step, kind).start()
    for kind in range(3):
        ycopy(2, kind).start()

    dqa[...] = jnp.zeros_like(dqa)
    dka[...] = jnp.zeros_like(dka)
    dva[...] = jnp.zeros_like(dva)
    def spread(slot):
        kt[slot] = kk[slot].astype(f32).T.astype(bf16)
        for h in range(HEADS):
            cols = slice(h * HEAD_DIM, h * HEAD_DIM + HEAD_DIM)
            km[slot, h] = kk[slot, :, cols]
            vm[slot, h] = vv[slot, :, cols]

    def arrive(what):
        for i in range(2):
            xcopy(what, i).wait_recv()

    def pass_on(hop):
        for kind in range(3):
            for way in range(2):
                ring(hop - 1, kind, way).wait_recv()
                ring(hop, kind, way).start()

    def y_arrive(step):
        for kind in range(3):
            ycopy(step, kind).wait_recv()

    def send_back(hop, way):
        if hop == 0:
            rows = slice(way * BLOCK, way * BLOCK + BLOCK)
            ring_out[0, way, rows] = (dqa[4, rows] * SCALING).astype(bf16)
        else:
            total = dqa[4 - hop if way == 0 else 4 + hop] * SCALING
            if hop > 1:
                ring_back(hop - 1, way).wait_recv()
                total = total + ring_in[hop - 1, way].astype(f32)
            ring_out[hop, way] = total.astype(bf16)
        if hop == 3:
            rows = slice(way * BLOCK, way * BLOCK + BLOCK)
            rest = slice(BLOCK - way * BLOCK, ROWS - way * BLOCK)
            ring_back(0, way).wait_recv()
            ring_out[3, way, rows] = (total[rows] + ring_in[0, way, rows].astype(f32)).astype(bf16)
            ring_out[3, way, rest] = total[rest].astype(bf16)
        ring_back(hop, way).start()

    def y_send_back(step, half=None):
        rows = slice(None) if half is None else slice(half * BLOCK, half * BLOCK + BLOCK)
        y_out[step - 1, rows] = (dqa[N_Z - 1 + step, rows] * SCALING).astype(bf16)
        y_back(step, half).start()

    def x_send_back(what, number, slot):
        x_out[number, 0] = (dka[slot] * SCALING).astype(bf16)
        x_back(what, 0).start()
        x_out[number, 1] = dva[slot].astype(bf16)
        x_back(what, 1).start()

    def far_send_back():
        x_back("pass", 0).wait_recv()
        x_out[3, 0] = (dka[3] * SCALING + x_in[2, 0].astype(f32)).astype(bf16)
        x_back("far", 0).start()
        x_back("pass", 1).wait_recv()
        x_out[3, 1] = (dva[3] + x_in[2, 1].astype(f32)).astype(bf16)
        x_back("far", 1).start()

    def at_1():
        arrive("near")
        for i in range(2):
            xcopy("far", i).start()
        pass_on(1)
        spread(1)

    def at_4():
        pass_on(2)

    def at_5():
        arrive("far")
        for i in range(2):
            xcopy("on", i).start()
        spread(3)

    def at_6():
        arrive("on")
        spread(4)

    def at_7():
        y_arrive(3)

    def at_8():
        pass_on(3)
        y_arrive(1)

    def at_10():
        send_back(1, 0)

    def at_11():
        send_back(1, 1)
        for kind in range(3):
            for way in range(2):
                ring(3, kind, way).wait_recv()

    def at_12():
        x_send_back("near", 0, 1)
        send_back(0, 0)
        send_back(0, 1)
        y_arrive(2)

    def at_13():
        x_send_back("pass", 2, 4)
        send_back(2, 0)
        send_back(2, 1)

    def at_14():
        far_send_back()
        y_send_back(2)

    def at_15():
        y_send_back(1)
        send_back(3, 0)
        send_back(3, 1)

    events = {
        1: at_1, 4: at_4, 5: at_5, 6: at_6, 7: at_7, 8: at_8, 10: at_10, 11: at_11, 12: at_12,
        13: at_13, 14: at_14, 15: at_15,
    }

    spread_loads = loads[3:5]
    for load in spread_loads:
        load.wait()
    spread(0)
    arrive("sib")
    spread(2)

    def table(s, values):
        if isinstance(s, int):
            return values[s]
        found = jnp.int32(values[0])
        for i, value in enumerate(values):
            if i > 0 and value != values[0]:
                found = jnp.where(s == i, jnp.int32(value), found)
        return found

    far_at = 32 + z * 4
    near_at = y * 8 + xh * 4
    across_at = y * 8 + (1 - xh) * 4
    one_lane = lax.broadcasted_iota(jnp.int32, (1, 128), 1)

    def step(s, carry):
        last = isinstance(s, int)
        for at, event in events.items():
            if not last:
                pl.when(s == at)(event)
            elif s == at:
                event()
        qd = table(s, [slot for slot, _ in STEPS])
        kind = table(s, [k for _, k in STEPS])
        key_slots = [table(s, [KEY_SLOTS[k][i] for _, k in STEPS]) for i in range(2)]
        start = near_at if last else jnp.where(kind == FAR, far_at, jnp.where(kind == NEAR, near_at, across_at))
        own = c if last else jnp.where(kind == FAR, xl, c)
        places_of = [start + own * 2, start + (1 - own) * 2]
        shown = meta[qd, 16:17, 0:128]
        hide = {}
        for i in range(2):
            for ke in range(2):
                cells = [
                    jnp.sum(jnp.where(one_lane == places_of[i] + (e * 64 + ke), shown, 0.0), axis=1, keepdims=True)
                    for e in range(2)
                ]
                hide[i, ke] = jnp.concatenate([jnp.broadcast_to(cell, (1, 128)) for cell in cells], axis=1)
        tiles = [(i, h) for h in range(HEADS) for i in range(2)]

        def first(tile):
            i, h = tile
            rows = slice(h * HEAD_DIM, h * HEAD_DIM + HEAD_DIM)
            return (
                dot(km[key_slots[i], h], qt[qd, rows, :], NN),
                dot(vm[key_slots[i], h], gt[qd, rows, :], NN),
            )

        def second(tile, scores, grad_p):
            i, h = tile
            lse, delta = meta[qd, h:h + 1, :], meta[qd, HEADS + h:HEADS + h + 1, :]
            low, grads = [], []
            for ke in range(2):
                rows = slice(ke * BLOCK, ke * BLOCK + BLOCK)
                attention = jnp.exp2(scores[rows] * (SCALING * LOG2E) - (lse + hide[i, ke]))
                low.append(attention.astype(bf16))
                grads.append((attention * (grad_p[rows] - delta)).astype(bf16))
            return jnp.concatenate(low, axis=0), jnp.concatenate(grads, axis=0)

        def third(tile, low, grads):
            i, h = tile
            rows = slice(h * HEAD_DIM, h * HEAD_DIM + HEAD_DIM)
            dva[key_slots[i], rows] += dot(gt[qd, rows, :], low, NT)
            dka[key_slots[i], rows] += dot(qt[qd, rows, :], grads, NT)
            dqa[qd, rows] += dot(kt[key_slots[i], rows, :], grads, NN)

        ones, twos = {}, {}
        for n in range(len(tiles) + 2):
            if n < len(tiles):
                ones[n] = first(tiles[n])
            if 0 <= n - 1 < len(tiles):
                twos[n - 1] = second(tiles[n - 1], *ones.pop(n - 1))
            if 0 <= n - 2 < len(tiles):
                third(tiles[n - 2], *twos.pop(n - 2))
            if last and n - 2 == len(tiles) // 2 - 1:
                y_send_back(3, 0)
        return carry

    lax.fori_loop(0, len(STEPS) - 1, step, 0)
    step(len(STEPS) - 1, 0)

    y_send_back(3, 1)
    x_send_back("sib", 1, 2)
    for i, own in enumerate((dka, dva)):
        total = own[0] * SCALING if i == 0 else own[0]
        for number, what in ((0, "near"), (1, "sib"), (3, "far")):
            x_back(what, i).wait_recv()
            total = total + x_in[number, i].astype(f32)
        sums[1 + i] = total.T.astype(bf16)
    total = dqa[0] * SCALING
    y_back(2).wait_recv()
    y_back(1).wait_recv()
    total = total + y_in[0].astype(f32) + y_in[1].astype(f32)
    for way in range(2):
        ring_back(3, way).wait_recv()
        total = total + ring_in[3, way].astype(f32)
    for half in range(2):
        y_back(3, half).wait_recv()
    total = total + y_in[2].astype(f32)
    sums[0] = total.astype(bf16)

    for hop in range(4):
        for way in range(2):
            for kind in range(3):
                ring(hop, kind, way).wait_send()
            ring_back(hop, way).wait_send()
    for s in (1, 2, 3):
        for kind in range(3):
            ycopy(s, kind).wait_send()
    y_back(1).wait_send()
    y_back(2).wait_send()
    for half in range(2):
        y_back(3, half).wait_send()
    for i in range(2):
        for what in ("near", "sib", "far", "on"):
            xcopy(what, i).wait_send()
        for what in ("near", "sib", "pass", "far"):
            x_back(what, i).wait_send()


def turn_kernel(sums, q_out, k_out, v_out):
    q_out[...] = sums[0].astype(jnp.float32).T.astype(jnp.bfloat16)
    k_out[...] = sums[1]
    v_out[...] = sums[2]


def body(
    queries, key_rows, value_rows, saved_output, output_grad, log_norm,
    local_lists, expander_lists, local_counts, expander_counts,
):
    bf16, f32 = jnp.bfloat16, jnp.float32
    dma = pltpu.SemaphoreType.DMA
    tile = (ROWS, D)
    sums = pl.pallas_call(
        kernel,
        name="backward",
        out_shape=jax.ShapeDtypeStruct((3, *tile), bf16),
        in_specs=[ANY] * 8 + [SMEM] * 2,
        out_specs=VMEM,
        scratch_shapes=[
            pltpu.VMEM(log_norm.shape, f32), pltpu.SMEM(local_lists.shape, jnp.int32),
            pltpu.SMEM(expander_lists.shape, jnp.int32),
            pltpu.VMEM(tile, bf16), pltpu.VMEM(tile, bf16), pltpu.VMEM(tile, bf16),
            pltpu.VMEM((Q_SLOTS, *tile), bf16), pltpu.VMEM((Q_SLOTS, *tile), bf16),
            pltpu.VMEM((Q_SLOTS, META, ROWS), f32),
            pltpu.VMEM((K_SLOTS, *tile), bf16), pltpu.VMEM((K_SLOTS, *tile), bf16),
            pltpu.VMEM((K_SLOTS, HEADS, ROWS, HEAD_DIM), bf16), pltpu.VMEM((K_SLOTS, HEADS, ROWS, HEAD_DIM), bf16),
            pltpu.VMEM((K_SLOTS, *tile), bf16),
            pltpu.VMEM((Q_SLOTS, *tile), f32),
            pltpu.VMEM((K_SLOTS, *tile), f32), pltpu.VMEM((K_SLOTS, *tile), f32),
            pltpu.VMEM((4, 2, *tile), bf16), pltpu.VMEM((4, 2, *tile), bf16),
            pltpu.VMEM((3, *tile), bf16), pltpu.VMEM((3, *tile), bf16),
            pltpu.VMEM((4, 2, *tile), bf16), pltpu.VMEM((4, 2, *tile), bf16),
            dma((8,)),
            dma((4, 3, 2)), dma((4, 3, 2)), dma((3, 3)), dma((3, 3)), dma((4, 2)), dma((4, 2)),
            dma((4, 2)), dma((4, 2)), dma((3, 2)), dma((3, 2)), dma((4, 2)), dma((4, 2)),
        ],
        compiler_params=pltpu.CompilerParams(
            collective_id=0, has_side_effects=True, vmem_limit_bytes=VMEM_LIMIT
        ),
    )(
        queries, output_grad, saved_output, key_rows, value_rows, log_norm,
        local_lists, expander_lists, local_counts, expander_counts,
    )
    return tuple(pl.pallas_call(
        turn_kernel,
        name="turn",
        out_shape=[jax.ShapeDtypeStruct(tile, bf16)] * 3,
        in_specs=[VMEM],
        out_specs=[VMEM] * 3,
    )(sums))


def solution(mesh):
    rows = P(("grp", "dom"), None)
    flat = P(("grp", "dom"))
    return jax.shard_map(
        body,
        mesh=mesh,
        in_specs=(rows, rows, rows, rows, rows, P(None, ("grp", "dom")), rows, rows, flat, flat),
        out_specs=(rows, rows, rows),
        check_vma=False,
    )
```

```python
import math

import jax
import jax.numpy as jnp
from jax import lax
from jax.experimental import pallas as pl
from jax.experimental.pallas import tpu as pltpu
from jax.sharding import PartitionSpec as P

HEADS = 8
HEAD_DIM = 32
BLOCK = 128
ROWS = 256
D = 256
N_Z, N_Y = 8, 4
Q_SLOTS = 11
K_SLOTS = 5
META = 24
HIDE = 1e30
SCALING = 1.0 / math.sqrt(HEAD_DIM)
LOG2E = math.log2(math.e)
MESH = pl.DeviceIdType.MESH
ANY = pl.BlockSpec(memory_space=pl.ANY)
VMEM = pl.BlockSpec(memory_space=pltpu.VMEM)
SMEM = pl.BlockSpec(memory_space=pltpu.SMEM)
VMEM_LIMIT = 56 * 1024 * 1024
FAR, NEAR, ACROSS = 0, 1, 2
STEPS = (
    (0, NEAR), (0, FAR), (1, FAR), (7, FAR), (2, FAR), (6, FAR), (0, ACROSS), (8, ACROSS),
    (10, ACROSS), (3, FAR), (5, FAR), (4, FAR), (9, ACROSS), (9, NEAR), (8, NEAR), (10, NEAR),
)
KEY_SLOTS = {FAR: (0, 1), NEAR: (0, 2), ACROSS: (3, 4)}
NT = (((1,), (1,)), ((), ()))
NN = (((1,), (0,)), ((), ()))


def dot(a, b, dims):
    return lax.dot_general(a, b, dims, preferred_element_type=jnp.float32)


def places():
    g, m = lax.axis_index("grp"), lax.axis_index("dom")
    return g // 4, g // 2 % 2, g % 2, m // 2, m % 2


def partners(y, xh, c, z, xl):
    def at(y=y, xh=xh, c=c, z=z, xl=xl):
        return ((y * 2 + xh) * 2 + c, z * 2 + xl)

    return {
        "right": at(z=(z + 1) % N_Z),
        "left": at(z=(z + N_Z - 1) % N_Z),
        "right3": at(z=(z + 3) % N_Z),
        "left3": at(z=(z + N_Z - 3) % N_Z),
        "y1": at(y=(y + 1) % N_Y),
        "y2": at(y=(y + 2) % N_Y),
        "y3": at(y=(y + 3) % N_Y),
        "far_x": at(xh=1 - xh),
        "near_x": at(xl=1 - xl),
        "sibling": at(c=1 - c),
    }


def kernel(
    q_ref, g_ref, o_ref, k_ref, v_ref, lse_hbm, ll_hbm, el_hbm, lc_hbm, ec_hbm,
    sums,
    lse_ref, ll_ref, el_ref, lc_ref, ec_ref,
    qb, gb, ob, qt, gt, meta, kk, vv, km, vm, kt, dqa, dka, dva,
    ring_out, ring_in, y_out, y_in, x_out, x_in,
    in_sem, ring_send, ring_recv, y_send, y_recv, x_send, x_recv,
    rr_send, rr_recv, ry_send, ry_recv, rx_send, rx_recv,
):
    y, xh, c, z, xl = places()
    others = partners(y, xh, c, z, xl)
    f32, bf16 = jnp.float32, jnp.bfloat16

    def remote(src, dst, send, recv, who):
        return pltpu.make_async_remote_copy(
            src_ref=src, dst_ref=dst, send_sem=send, recv_sem=recv,
            device_id=others[who], device_id_type=MESH,
        )

    held = (qt, gt, meta)
    halves = ((0, BLOCK), (0, BLOCK), (0, 16))
    sizes = ((BLOCK, BLOCK), (BLOCK, BLOCK), (16, 8))

    def ring(hop, kind, way):
        whole = held[kind]
        src, dst = ((N_Z - hop) % N_Z, N_Z - 1 - hop) if way == 0 else (hop, hop + 1)
        src, dst = whole.at[src], whole.at[dst]
        if hop == 3:
            start = 0 if way == 0 else sizes[kind][0]
            rows = pl.ds(start, sizes[kind][way])
            src, dst = src.at[rows], dst.at[rows]
        return remote(
            src, dst, ring_send.at[hop, kind, way], ring_recv.at[hop, kind, way],
            "right" if way == 0 else "left",
        )

    def ycopy(step, kind):
        whole = held[kind]
        return remote(
            whole.at[0], whole.at[N_Z - 1 + N_Y - step], y_send.at[step - 1, kind],
            y_recv.at[step - 1, kind], f"y{step}",
        )

    def xcopy(what, i):
        whole, own = (kk, k_ref) if i == 0 else (vv, v_ref)
        number, who = {"near": (0, "near_x"), "sib": (1, "sibling"), "far": (2, "far_x"), "on": (3, "sibling")}[what]
        src = whole.at[3] if what == "on" else own
        return remote(src, whole.at[number + 1], x_send.at[number, i], x_recv.at[number, i], who)

    def ring_back(hop, way):
        buf, into = ring_out.at[hop, way], ring_in.at[hop, way]
        if hop == 0:
            rows = pl.ds(way * BLOCK, BLOCK)
            buf, into = buf.at[rows], into.at[rows]
        who = ("right", "left")[way] + ("3" if hop == 0 else "")
        return remote(buf, into, rr_send.at[hop, way], rr_recv.at[hop, way], who)

    def y_back(step, half=None):
        buf, into = y_out.at[step - 1], y_in.at[step - 1]
        if half is not None:
            rows = pl.ds(half * BLOCK, BLOCK)
            buf, into = buf.at[rows], into.at[rows]
        at = (step - 1, half or 0)
        return remote(buf, into, ry_send.at[at], ry_recv.at[at], f"y{step}")

    def x_back(what, i):
        number, who = {"near": (0, "near_x"), "sib": (1, "sibling"), "pass": (2, "sibling"), "far": (3, "far_x")}[what]
        return remote(x_out.at[number, i], x_in.at[number, i], rx_send.at[number, i], rx_recv.at[number, i], who)

    barrier = pltpu.get_barrier_semaphore()
    for device in others.values():
        pl.semaphore_signal(barrier, inc=1, device_id=device, device_id_type=MESH)
    loads = [
        pltpu.make_async_copy(src, dst, in_sem.at[i])
        for i, (src, dst) in enumerate(
            (
                (q_ref, qb), (g_ref, gb), (o_ref, ob), (k_ref, kk.at[0]), (v_ref, vv.at[0]),
                (lse_hbm, lse_ref), (ll_hbm, ll_ref), (el_hbm, el_ref),
                (lc_hbm, lc_ref), (ec_hbm, ec_ref),
            )
        )
    ]
    for load in loads:
        load.start()

    lane = lax.broadcasted_iota(jnp.int32, (8, 128), 1)

    def mark(lists, counts, e, base):
        def one(s, hidden):
            hit = (lane == base + lists[e, s]) & (s < counts[e])
            return jnp.where(hit, 0.0, hidden)
        return one

    for load in loads[5:]:
        load.wait()
    hidden = jnp.full((8, 128), HIDE, f32)
    for e in range(2):
        hidden = lax.fori_loop(0, ll_ref.shape[1], mark(ll_ref, lc_ref, e, e * 64), hidden)
        hidden = lax.fori_loop(0, el_ref.shape[1], mark(el_ref, ec_ref, e, e * 64 + 32), hidden)
    meta[0, 16:24, 0:128] = hidden
    meta[0, 16:24, 128:256] = hidden
    meta[0, 0:HEADS, :] = lse_ref[...] * LOG2E

    loads[0].wait()
    qt[0] = qb[...].astype(f32).T.astype(bf16)
    loads[1].wait()
    gt[0] = gb[...].astype(f32).T.astype(bf16)
    loads[2].wait()
    product = gb[...].astype(f32) * ob[...].astype(f32)
    high = product.astype(bf16)
    low = (product - high.astype(f32)).astype(bf16)
    rows_of = lax.broadcasted_iota(jnp.int32, (HEADS, D), 0)
    cols_of = lax.broadcasted_iota(jnp.int32, (HEADS, D), 1)
    pick = jnp.where(cols_of // HEAD_DIM == rows_of, 1.0, 0.0).astype(bf16)
    meta[0, HEADS:2 * HEADS, :] = dot(pick, high, NT) + dot(pick, low, NT)

    pl.semaphore_wait(barrier, len(others))
    for i in range(2):
        for what in ("near", "sib"):
            xcopy(what, i).start()
    for kind in range(3):
        for way in range(2):
            ring(0, kind, way).start()
        for step in (1, 3):
            ycopy(step, kind).start()
    for kind in range(3):
        ycopy(2, kind).start()

    dqa[...] = jnp.zeros_like(dqa)
    dka[...] = jnp.zeros_like(dka)
    dva[...] = jnp.zeros_like(dva)
    def spread(slot):
        kt[slot] = kk[slot].astype(f32).T.astype(bf16)
        for h in range(HEADS):
            cols = slice(h * HEAD_DIM, h * HEAD_DIM + HEAD_DIM)
            km[slot, h] = kk[slot, :, cols]
            vm[slot, h] = vv[slot, :, cols]

    def arrive(what):
        for i in range(2):
            xcopy(what, i).wait_recv()

    def pass_on(hop):
        for kind in range(3):
            for way in range(2):
                ring(hop - 1, kind, way).wait_recv()
                ring(hop, kind, way).start()

    def y_arrive(step):
        for kind in range(3):
            ycopy(step, kind).wait_recv()

    def send_back(hop, way):
        if hop == 0:
            rows = slice(way * BLOCK, way * BLOCK + BLOCK)
            ring_out[0, way, rows] = (dqa[4, rows] * SCALING).astype(bf16)
        else:
            total = dqa[4 - hop if way == 0 else 4 + hop] * SCALING
            if hop > 1:
                ring_back(hop - 1, way).wait_recv()
                total = total + ring_in[hop - 1, way].astype(f32)
            ring_out[hop, way] = total.astype(bf16)
        if hop == 3:
            rows = slice(way * BLOCK, way * BLOCK + BLOCK)
            rest = slice(BLOCK - way * BLOCK, ROWS - way * BLOCK)
            ring_back(0, way).wait_recv()
            ring_out[3, way, rows] = (total[rows] + ring_in[0, way, rows].astype(f32)).astype(bf16)
            ring_out[3, way, rest] = total[rest].astype(bf16)
        ring_back(hop, way).start()

    def y_send_back(step, half=None):
        rows = slice(None) if half is None else slice(half * BLOCK, half * BLOCK + BLOCK)
        y_out[step - 1, rows] = (dqa[N_Z - 1 + step, rows] * SCALING).astype(bf16)
        y_back(step, half).start()

    def x_send_back(what, number, slot):
        x_out[number, 0] = (dka[slot] * SCALING).astype(bf16)
        x_back(what, 0).start()
        x_out[number, 1] = dva[slot].astype(bf16)
        x_back(what, 1).start()

    def far_send_back():
        x_back("pass", 0).wait_recv()
        x_out[3, 0] = (dka[3] * SCALING + x_in[2, 0].astype(f32)).astype(bf16)
        x_back("far", 0).start()
        x_back("pass", 1).wait_recv()
        x_out[3, 1] = (dva[3] + x_in[2, 1].astype(f32)).astype(bf16)
        x_back("far", 1).start()

    def at_1():
        arrive("near")
        for i in range(2):
            xcopy("far", i).start()
        pass_on(1)
        spread(1)

    def at_4():
        pass_on(2)

    def at_5():
        arrive("far")
        for i in range(2):
            xcopy("on", i).start()
        spread(3)

    def at_6():
        arrive("on")
        spread(4)

    def at_7():
        y_arrive(3)

    def at_8():
        pass_on(3)
        y_arrive(1)

    def at_10():
        send_back(1, 0)

    def at_11():
        send_back(1, 1)
        for kind in range(3):
            for way in range(2):
                ring(3, kind, way).wait_recv()

    def at_12():
        x_send_back("near", 0, 1)
        send_back(0, 0)
        send_back(0, 1)
        y_arrive(2)

    def at_13():
        x_send_back("pass", 2, 4)
        send_back(2, 0)
        send_back(2, 1)

    def at_14():
        far_send_back()
        y_send_back(2)

    def at_15():
        y_send_back(1)
        send_back(3, 0)
        send_back(3, 1)

    events = {
        1: at_1, 4: at_4, 5: at_5, 6: at_6, 7: at_7, 8: at_8, 10: at_10, 11: at_11, 12: at_12,
        13: at_13, 14: at_14, 15: at_15,
    }

    spread_loads = loads[3:5]
    for load in spread_loads:
        load.wait()
    spread(0)
    arrive("sib")
    spread(2)

    def table(s, values):
        if isinstance(s, int):
            return values[s]
        found = jnp.int32(values[0])
        for i, value in enumerate(values):
            if i > 0 and value != values[0]:
                found = jnp.where(s == i, jnp.int32(value), found)
        return found

    far_at = 32 + z * 4
    near_at = y * 8 + xh * 4
    across_at = y * 8 + (1 - xh) * 4
    one_lane = lax.broadcasted_iota(jnp.int32, (1, 128), 1)

    def step(s, carry):
        last = isinstance(s, int)
        for at, event in events.items():
            if not last:
                pl.when(s == at)(event)
            elif s == at:
                event()
        qd = table(s, [slot for slot, _ in STEPS])
        kind = table(s, [k for _, k in STEPS])
        key_slots = [table(s, [KEY_SLOTS[k][i] for _, k in STEPS]) for i in range(2)]
        start = near_at if last else jnp.where(kind == FAR, far_at, jnp.where(kind == NEAR, near_at, across_at))
        own = c if last else jnp.where(kind == FAR, xl, c)
        places_of = [start + own * 2, start + (1 - own) * 2]
        shown = meta[qd, 16:17, 0:128]
        hide = {}
        for i in range(2):
            for ke in range(2):
                cells = [
                    jnp.sum(jnp.where(one_lane == places_of[i] + (e * 64 + ke), shown, 0.0), axis=1, keepdims=True)
                    for e in range(2)
                ]
                hide[i, ke] = jnp.concatenate([jnp.broadcast_to(cell, (1, 128)) for cell in cells], axis=1)
        tiles = [(i, h) for h in range(HEADS) for i in range(2)]

        def first(tile):
            i, h = tile
            rows = slice(h * HEAD_DIM, h * HEAD_DIM + HEAD_DIM)
            return (
                dot(km[key_slots[i], h], qt[qd, rows, :], NN),
                dot(vm[key_slots[i], h], gt[qd, rows, :], NN),
            )

        def second(tile, scores, grad_p):
            i, h = tile
            lse, delta = meta[qd, h:h + 1, :], meta[qd, HEADS + h:HEADS + h + 1, :]
            low, grads = [], []
            for ke in range(2):
                rows = slice(ke * BLOCK, ke * BLOCK + BLOCK)
                attention = jnp.exp2(scores[rows] * (SCALING * LOG2E) - (lse + hide[i, ke]))
                low.append(attention.astype(bf16))
                grads.append((attention * (grad_p[rows] - delta)).astype(bf16))
            return jnp.concatenate(low, axis=0), jnp.concatenate(grads, axis=0)

        def third(tile, low, grads):
            i, h = tile
            rows = slice(h * HEAD_DIM, h * HEAD_DIM + HEAD_DIM)
            dva[key_slots[i], rows] += dot(gt[qd, rows, :], low, NT)
            dka[key_slots[i], rows] += dot(qt[qd, rows, :], grads, NT)
            dqa[qd, rows] += dot(kt[key_slots[i], rows, :], grads, NN)

        ones, twos = {}, {}
        for n in range(len(tiles) + 2):
            if n < len(tiles):
                ones[n] = first(tiles[n])
            if 0 <= n - 1 < len(tiles):
                twos[n - 1] = second(tiles[n - 1], *ones.pop(n - 1))
            if 0 <= n - 2 < len(tiles):
                third(tiles[n - 2], *twos.pop(n - 2))
            if last and n - 2 == len(tiles) // 2 - 1:
                y_send_back(3, 0)
        return carry

    lax.fori_loop(0, len(STEPS) - 1, step, 0)
    step(len(STEPS) - 1, 0)

    y_send_back(3, 1)
    x_send_back("sib", 1, 2)
    for i, own in enumerate((dka, dva)):
        total = own[0] * SCALING if i == 0 else own[0]
        for number, what in ((0, "near"), (1, "sib"), (3, "far")):
            x_back(what, i).wait_recv()
            total = total + x_in[number, i].astype(f32)
        sums[1 + i] = total.T.astype(bf16)
    total = dqa[0] * SCALING
    y_back(2).wait_recv()
    y_back(1).wait_recv()
    total = total + y_in[0].astype(f32) + y_in[1].astype(f32)
    for way in range(2):
        ring_back(3, way).wait_recv()
        total = total + ring_in[3, way].astype(f32)
    for half in range(2):
        y_back(3, half).wait_recv()
    total = total + y_in[2].astype(f32)
    sums[0] = total.astype(bf16)

    for hop in range(4):
        for way in range(2):
            for kind in range(3):
                ring(hop, kind, way).wait_send()
            ring_back(hop, way).wait_send()
    for s in (1, 2, 3):
        for kind in range(3):
            ycopy(s, kind).wait_send()
    y_back(1).wait_send()
    y_back(2).wait_send()
    for half in range(2):
        y_back(3, half).wait_send()
    for i in range(2):
        for what in ("near", "sib", "far", "on"):
            xcopy(what, i).wait_send()
        for what in ("near", "sib", "pass", "far"):
            x_back(what, i).wait_send()


def turn_kernel(sums, q_out, k_out, v_out):
    q_out[...] = sums[0].astype(jnp.float32).T.astype(jnp.bfloat16)
    k_out[...] = sums[1]
    v_out[...] = sums[2]


def body(
    queries, key_rows, value_rows, saved_output, output_grad, log_norm,
    local_lists, expander_lists, local_counts, expander_counts,
):
    bf16, f32 = jnp.bfloat16, jnp.float32
    dma = pltpu.SemaphoreType.DMA
    tile = (ROWS, D)
    sums = pl.pallas_call(
        kernel,
        name="backward",
        out_shape=jax.ShapeDtypeStruct((3, *tile), bf16),
        in_specs=[ANY] * 10,
        out_specs=VMEM,
        scratch_shapes=[
            pltpu.VMEM(log_norm.shape, f32), pltpu.SMEM(local_lists.shape, jnp.int32),
            pltpu.SMEM(expander_lists.shape, jnp.int32),
            pltpu.SMEM(local_counts.shape, jnp.int32), pltpu.SMEM(expander_counts.shape, jnp.int32),
            pltpu.VMEM(tile, bf16), pltpu.VMEM(tile, bf16), pltpu.VMEM(tile, bf16),
            pltpu.VMEM((Q_SLOTS, *tile), bf16), pltpu.VMEM((Q_SLOTS, *tile), bf16),
            pltpu.VMEM((Q_SLOTS, META, ROWS), f32),
            pltpu.VMEM((K_SLOTS, *tile), bf16), pltpu.VMEM((K_SLOTS, *tile), bf16),
            pltpu.VMEM((K_SLOTS, HEADS, ROWS, HEAD_DIM), bf16), pltpu.VMEM((K_SLOTS, HEADS, ROWS, HEAD_DIM), bf16),
            pltpu.VMEM((K_SLOTS, *tile), bf16),
            pltpu.VMEM((Q_SLOTS, *tile), f32),
            pltpu.VMEM((K_SLOTS, *tile), f32), pltpu.VMEM((K_SLOTS, *tile), f32),
            pltpu.VMEM((4, 2, *tile), bf16), pltpu.VMEM((4, 2, *tile), bf16),
            pltpu.VMEM((3, *tile), bf16), pltpu.VMEM((3, *tile), bf16),
            pltpu.VMEM((4, 2, *tile), bf16), pltpu.VMEM((4, 2, *tile), bf16),
            dma((10,)),
            dma((4, 3, 2)), dma((4, 3, 2)), dma((3, 3)), dma((3, 3)), dma((4, 2)), dma((4, 2)),
            dma((4, 2)), dma((4, 2)), dma((3, 2)), dma((3, 2)), dma((4, 2)), dma((4, 2)),
        ],
        compiler_params=pltpu.CompilerParams(
            collective_id=0, has_side_effects=True, vmem_limit_bytes=VMEM_LIMIT
        ),
    )(
        queries, output_grad, saved_output, key_rows, value_rows, log_norm,
        local_lists, expander_lists, local_counts, expander_counts,
    )
    return tuple(pl.pallas_call(
        turn_kernel,
        name="turn",
        out_shape=[jax.ShapeDtypeStruct(tile, bf16)] * 3,
        in_specs=[VMEM],
        out_specs=[VMEM] * 3,
    )(sums))


def solution(mesh):
    rows = P(("grp", "dom"), None)
    flat = P(("grp", "dom"))
    return jax.shard_map(
        body,
        mesh=mesh,
        in_specs=(rows, rows, rows, rows, rows, P(None, ("grp", "dom")), rows, rows, flat, flat),
        out_specs=(rows, rows, rows),
        check_vma=False,
    )
```
